256 devices in a mesh: cache: 16 (over x, y), tensor: 16 (over z, core).
Axes of the slice: x: 4, y: 4, z: 8, core: 2. Of those that a mesh axis runs over, the one named last changes fastest.
Arguments:
- hidden: bfloat16 [128, 128, 2048], P('cache'), may hold values from -6 to 6
- lengths: int32 [128], replicated, may hold values from 1 to 128, 10240 in all
- owners: int32 [128], replicated, may hold values from 0 to 15, as said below
- slot_ids: int32 [128], replicated, may hold values from 0 to 15, as said below
- state_cache: float32 [256, 32, 128, 128], P('cache', 'tensor'), may hold values from -6 to 6
- conv_cache: bfloat16 [256, 3, 16, 512], P('cache', None, 'tensor'), may hold values from -6 to 6
- w_qkvz: bfloat16 [2048, 16, 768], P(None, 'tensor'), may hold values from -0.125 to 0.125
- w_beta_alpha: bfloat16 [2048, 16, 4], P(None, 'tensor'), may hold values from -0.125 to 0.125
- conv_weight: bfloat16 [4, 16, 512], P(None, 'tensor'), may hold values from -3 to 3
- decay_log: float32 [32], P('tensor'), may hold values from -1 to 2
- step_bias: float32 [32], P('tensor'), may hold values from -6 to -4
- norm_gain: float32 [128], replicated, may hold values from 0.1 to 1.9
- w_out: bfloat16 [4096, 2048], P('tensor'), may hold values from -0.125 to 0.125
Outputs:
- layer_out: bfloat16 [128, 128, 2048], P('cache', None, 'tensor')
- new_state_cache: float32 [256, 32, 128, 128], P('cache', 'tensor')
- new_conv_cache: bfloat16 [256, 3, 16, 512], P('cache', None, 'tensor')
The draws below stay inside these ranges and needn't reach their ends.
Inputs may be any that keep to these rules, and one draw needn't show every extreme that they name: `owners`: no two conversations share an owner and a slot. At most 16 conversations have one owner, and one owner has exactly that many; among the 8 conversations of one index of the cache axis at most 1 have one owner, and some have exactly that many. Every owner holds at least one conversation. `slot_ids`: slots of one owner's conversations are distinct.
All inputs are finite; a program needn't handle non-finite values.
Results may differ from the reference program's by a relative error of at most 0.009.
Values may be sent and summed in bfloat16 or wider, within the bound.
A program may use at most 128 MiB of HBM per device.

```python
import math
import jax
import jax.numpy as jnp
import numpy as np
from jax import lax

D = 2048
HV = 32
HK = 16
DK = 128
DV = 128
CONV_K = 4
NEW = 128
BLOCK = 64
CONV_DEV = 8
GROUP = 2
CH = 512
QKVZ = 768
SLOTS_PER_SHARD = 16
SLOTS = 256
DIALOGUE_TOTAL = 128


def route_tables(key):
    holder_count = DIALOGUE_TOTAL // CONV_DEV
    pool_size = holder_count * SLOTS_PER_SHARD
    key_heat, key_hot, key_pick, key_order, slot_key_value = jax.random.split(key, 5)
    heat_levels = jax.random.randint(key_heat, (holder_count,), 0, 4)
    hot_owner = jax.random.randint(key_hot, (), 0, holder_count)
    pool_ids = jnp.arange(pool_size, dtype=jnp.int32)
    holder_lookup = pool_ids // SLOTS_PER_SHARD
    position_lookup = pool_ids % SLOTS_PER_SHARD
    scores = jax.random.randint(key_pick, (pool_size,), 0, 1024) + heat_levels[holder_lookup] * 512
    scores = scores + jnp.where(holder_lookup == hot_owner, 8192, 0) + jnp.where(position_lookup == 0, 4096, 0)
    scores = scores * pool_size + pool_ids
    selected_pick = jnp.sort(lax.top_k(scores, DIALOGUE_TOTAL)[1])
    position = jnp.arange(DIALOGUE_TOTAL, dtype=jnp.int32)
    block_of = position % holder_count
    within = position // holder_count
    shuffle = jnp.argsort(jax.random.randint(key_order, (holder_count, CONV_DEV), 0, 65536) * CONV_DEV + jnp.arange(CONV_DEV, dtype=jnp.int32)[None, :], axis=1).astype(jnp.int32)
    dialogue_index = block_of * CONV_DEV + shuffle[block_of, within]
    relabel_slots = jnp.argsort(jax.random.randint(slot_key_value, (holder_count, SLOTS_PER_SHARD), 0, 65536) * SLOTS_PER_SHARD + jnp.arange(SLOTS_PER_SHARD, dtype=jnp.int32)[None, :], axis=1).astype(jnp.int32)
    owner_list = jnp.zeros((DIALOGUE_TOTAL,), jnp.int32).at[dialogue_index].set(holder_lookup[selected_pick])
    slot_sequence = jnp.zeros((DIALOGUE_TOTAL,), jnp.int32).at[dialogue_index].set(relabel_slots[holder_lookup[selected_pick], position_lookup[selected_pick]])
    return (owner_list, slot_sequence)


def draw_owners(key, part):
    return route_tables(key)[0]


def draw_slot_ids(key, part):
    return route_tables(key)[1]


def strengthened(result, key, source, target, blocks, factor):
    owner, partner = [(jnp.arange(result.shape[axis_at]) // (result.shape[axis_at] // blocks)).reshape([-1 if axis == axis_at else 1 for axis in range(result.ndim)]) for axis_at in (source, target)]
    chosen = jax.random.permutation(key, blocks)[partner]
    strong = (owner == chosen) | (owner == (partner + blocks // 2) % blocks)
    return jnp.where(strong, factor * result, result)


def steps_of(stream_key, shape, shards, low, top_value):
    loudness, own = 1.0, jax.random.fold_in(stream_key, 6)
    for dim, parts in shards:
        heights = jnp.exp(jax.random.uniform(jax.random.fold_in(own, dim), (parts,), jnp.float32, low / len(shards), top_value / len(shards)))
        loudness = loudness * jnp.repeat(heights, shape[dim] // parts).reshape([-1 if axis == dim else 1 for axis in range(len(shape))])
    return loudness


def length_profile(count, total, reach, slope):
    weights = [(1 << 20) // math.isqrt(rank ** slope) + 1 for rank in range(2, count + 1)]
    spare, counts = total - reach - (count - 1), [1] * (count - 1)
    while spare > 0:
        movable = [i for i in range(count - 1) if counts[i] < reach]
        pool, remaining = sum([weights[i] for i in movable]), spare
        for i in movable:
            addition = min(reach - counts[i], max(1, remaining * weights[i] // pool), spare)
            counts[i] = counts[i] + addition
            spare = spare - addition
    return np.array([reach] + counts)


def uneven(key, count, total, bound, skew):
    if count == 2:
        one = jax.random.randint(key, (), max(1, total - bound), min(bound, total - 1) + 1)
        return jnp.stack([one, total - one])
    sizes = jnp.asarray(length_profile(count, total, bound, skew), jnp.int32)
    twos = (count - 1) // 2
    source_of, sink = sizes[1:1 + 2 * twos:2], sizes[2:2 + 2 * twos:2]
    margin = jnp.minimum(source_of - 1, bound - sink)
    shifted = jax.random.randint(jax.random.fold_in(key, 1), (twos,), 0, 1 << 20) % (margin + 1)
    sizes = sizes.at[1:1 + 2 * twos:2].set(source_of - shifted).at[2:2 + 2 * twos:2].set(sink + shifted)
    return sizes[jax.random.permutation(jax.random.fold_in(key, 2), count)]


def noise(own_key, shape, spread, reach, cuts=(), kind=jnp.bfloat16):
    loudness = steps_of(own_key, shape, cuts, -0.22, 0.18) if cuts else 1.0
    values = jax.random.normal(own_key, shape, jnp.float32) * spread * loudness
    return jnp.minimum(jnp.maximum(values, -reach), reach).astype(kind)


def bell_draw_with(key, shape, width, most, cuts, heavy, kind=jnp.bfloat16):
    array = width * jax.random.normal(key, shape, jnp.float32)
    if cuts:
        array = array * steps_of(key, shape, cuts, -0.22, 0.18)
    return jnp.clip(strengthened(array, jax.random.fold_in(key, 3), *heavy), -most, most).astype(kind)


def setup_inputs(seed: int = 0) -> dict:
    splits = jax.random.split(jax.random.key(seed), 14)
    return {
        "hidden": noise(splits[0], (DIALOGUE_TOTAL, NEW, D), 1.0, 6.0, ((0, 16),)),
        "lengths": uneven(splits[1], DIALOGUE_TOTAL, DIALOGUE_TOTAL * NEW * 5 // 8, NEW, 1).astype(jnp.int32),
        "owners": draw_owners(jax.random.fold_in(splits[13], 71), 0),
        "slot_ids": draw_slot_ids(jax.random.fold_in(splits[13], 71), 0),
        "state_cache": noise(splits[4], (SLOTS, HV, DK, DV), 1.0, 6.0, ((0, 16), (1, 16)), jnp.float32),
        "conv_cache": noise(splits[5], (SLOTS, CONV_K - 1, HK, CH), 1.0, 6.0, ((0, 16), (2, 16))),
        "w_qkvz": noise(splits[6], (D, HK, QKVZ), D ** -0.5, 0.125, ((1, 16),)),
        "w_beta_alpha": noise(splits[7], (D, HK, 2 * GROUP), D ** -0.5, 0.125, ((1, 16),)),
        "conv_weight": noise(splits[8], (CONV_K, HK, CH), 0.5, 3.0, ((1, 16),)),
        "decay_log": jnp.clip(-1.0 + 3.0 * jax.random.uniform(splits[9], (HV,), jnp.float32) ** steps_of(splits[9], (HV,), ((0, 16),), -0.2, 0.2), -1.0, 2.0),
        "step_bias": jnp.clip(-6.0 + 2.0 * jax.random.uniform(splits[10], (HV,), jnp.float32) ** steps_of(splits[10], (HV,), ((0, 16),), -0.2, 0.2), -6.0, -4.0),
        "norm_gain": jnp.clip(1.0 + 0.18 * jax.random.normal(splits[11], (DV,), jnp.float32), 0.1, 1.9),
        "w_out": bell_draw_with(splits[12], (HV * DV, D), (HV * DV) ** -0.5, 0.125, ((0, 16),), (0, 1, 16, 2.0)),
    }


HIGHEST_PREC = lax.Precision.HIGHEST

def unit_lower_inverse(lower_part):
    span = lower_part.shape[-1]
    identity_mat = jnp.eye(span, dtype=lower_part.dtype)
    power = -lower_part
    inverse = identity_mat + power
    for level in range((span - 1).bit_length() - 1):
        power = jnp.einsum('...ij,...jk->...ik', power, power, precision=HIGHEST_PREC)
        inverse = inverse + jnp.einsum('...ij,...jk->...ik', inverse, power, precision=HIGHEST_PREC)
    return inverse

def block_step(memory, block_in):
    queries, key_rows, values, decays, beta_gate = block_in
    span = decays.shape[-1]
    cumulative = jnp.cumsum(decays, axis=-1)
    row_ids = lax.broadcasted_iota(jnp.int32, (span, span), 0)
    col_ids = lax.broadcasted_iota(jnp.int32, (span, span), 1)
    inclusive = row_ids >= col_ids
    strictly = row_ids > col_ids
    log_gaps = cumulative[..., :, None] - cumulative[..., None, :]
    weighting = jnp.where(inclusive, jnp.exp(jnp.where(inclusive, log_gaps, 0.0)), 0.0)
    key_intersection = jnp.einsum('...id,...jd->...ij', key_rows, key_rows, precision=HIGHEST_PREC)
    lower_part = jnp.where(strictly, beta_gate[..., :, None] * key_intersection * weighting, 0.0)
    growth = jnp.exp(cumulative)
    right_side = jnp.concatenate([(beta_gate * growth)[..., None] * key_rows, beta_gate[..., None] * values], axis=-1)
    inverse = unit_lower_inverse(lower_part)
    solved = jnp.einsum('...ij,...jk->...ik', inverse, right_side, precision=HIGHEST_PREC)
    key_dim = key_rows.shape[-1]
    updates = solved[..., key_dim:] - jnp.einsum('...ld,...de->...le', solved[..., :key_dim], memory, precision=HIGHEST_PREC)
    scores = jnp.einsum('...id,...jd->...ij', queries, key_rows, precision=HIGHEST_PREC) * weighting
    outputs = jnp.einsum('...ld,...de->...le', queries * growth[..., None], memory, precision=HIGHEST_PREC)
    outputs = outputs + jnp.einsum('...ij,...je->...ie', scores, updates, precision=HIGHEST_PREC)
    final_log = cumulative[..., -1:]
    fading = jnp.exp(final_log - cumulative)
    memory = jnp.exp(final_log)[..., None] * memory + jnp.einsum('...ld,...le->...de', key_rows * fading[..., None], updates, precision=HIGHEST_PREC)
    return (memory, outputs)

def delta_rule(memory, queries, key_rows, values, decays, beta_gate):
    positions = decays.shape[-1]
    block_count = positions // BLOCK

    def to_blocks(array_in):
        shaped = array_in.reshape(array_in.shape[:-2] + (block_count, BLOCK, array_in.shape[-1]))
        return jnp.moveaxis(shaped, -3, 0)

    def to_blocks_flat(array_in):
        shaped = array_in.reshape(array_in.shape[:-1] + (block_count, BLOCK))
        return jnp.moveaxis(shaped, -2, 0)
    final_memory, outputs = lax.scan(block_step, memory, (to_blocks(queries), to_blocks(key_rows), to_blocks(values), to_blocks_flat(decays), to_blocks_flat(beta_gate)))
    outputs = jnp.moveaxis(outputs, 0, -3)
    outputs = outputs.reshape(outputs.shape[:-3] + (positions, outputs.shape[-1]))
    return (final_memory, outputs)

def project(hidden, w_qkvz, w_beta_alpha):
    model_dim = hidden.shape[-1]
    flat_rows = hidden.reshape(-1, model_dim)
    projected = jnp.dot(flat_rows, w_qkvz.reshape(model_dim, -1), preferred_element_type=jnp.float32).astype(jnp.bfloat16)
    gate_raw = jnp.dot(flat_rows, w_beta_alpha.reshape(model_dim, -1), preferred_element_type=jnp.float32).astype(jnp.bfloat16)
    lead_shape = hidden.shape[:-1]
    return (projected.reshape(lead_shape + w_qkvz.shape[1:]), gate_raw.reshape(lead_shape + w_beta_alpha.shape[1:]))

def advance(projected, gate_raw, lengths, memory, conv_state, conv_weight, decay_log, step_bias, norm_gain):
    items = projected.shape[0]
    new_tokens = projected.shape[1]
    key_heads = projected.shape[2]
    value_heads = memory.shape[1]
    key_dim = memory.shape[2]
    value_dim = memory.shape[3]
    group_size = value_heads // key_heads
    channels = conv_state.shape[-1]
    tap_count = conv_weight.shape[0]
    mixed_part = projected[..., :channels]
    z_part = projected[..., channels:]
    extended = jnp.concatenate([conv_state, mixed_part], axis=1)
    convolved = jnp.zeros((items, new_tokens, key_heads, channels), jnp.float32)
    for offset in range(tap_count):
        convolved = convolved + conv_weight[offset].astype(jnp.float32) * extended[:, offset:offset + new_tokens].astype(jnp.float32)
    activated = jax.nn.silu(convolved)
    tail_rows = jax.vmap(lambda rows_in, first_row: lax.dynamic_slice_in_dim(rows_in, first_row, tap_count - 1, 0))(extended, lengths.astype(jnp.int32))
    queries = activated[..., :key_dim]
    queries = queries * lax.rsqrt(lax.optimization_barrier(jnp.sum(queries * queries, axis=-1, keepdims=True)) + 1e-06) * (1.0 / math.sqrt(key_dim))
    key_rows = activated[..., key_dim:2 * key_dim]
    key_rows = key_rows * lax.rsqrt(lax.optimization_barrier(jnp.sum(key_rows * key_rows, axis=-1, keepdims=True)) + 1e-06)
    values = activated[..., 2 * key_dim:].reshape(items, new_tokens, value_heads, value_dim)
    queries = jnp.repeat(queries, group_size, axis=2)
    key_rows = jnp.repeat(key_rows, group_size, axis=2)
    gate_vals = gate_raw.astype(jnp.float32)
    beta_logit = gate_vals[..., :group_size].reshape(items, new_tokens, value_heads)
    decay_input = gate_vals[..., group_size:].reshape(items, new_tokens, value_heads)
    live_mask = jnp.arange(new_tokens, dtype=jnp.int32)[None, :] < lengths.astype(jnp.int32)[:, None]
    beta_gate = jnp.where(live_mask[..., None], jax.nn.sigmoid(beta_logit), 0.0)
    decays = jnp.where(live_mask[..., None], -jnp.exp(decay_log) * jax.nn.softplus(decay_input + step_bias), 0.0)
    final_memory, core = delta_rule(memory, queries.transpose(0, 2, 1, 3), key_rows.transpose(0, 2, 1, 3), values.transpose(0, 2, 1, 3), decays.transpose(0, 2, 1), beta_gate.transpose(0, 2, 1))
    core = core.transpose(0, 2, 1, 3)
    z_gate = z_part.astype(jnp.float32).reshape(items, new_tokens, value_heads, value_dim)
    normed = core * lax.rsqrt(lax.optimization_barrier(jnp.mean(core * core, axis=-1, keepdims=True)) + 1e-06) * norm_gain * jax.nn.silu(z_gate)
    normed = jnp.where(live_mask[..., None, None], normed, 0.0).astype(jnp.bfloat16)
    return (normed.reshape(items, new_tokens, value_heads * value_dim), final_memory, tail_rows)

def reference(hidden, lengths, owners, slot_ids, state_cache, conv_cache, w_qkvz, w_beta_alpha, conv_weight, decay_log, step_bias, norm_gain, w_out):
    cache_index = (owners * SLOTS_PER_SHARD + slot_ids).astype(jnp.int32)
    memories = state_cache[cache_index]
    conv_states = conv_cache[cache_index]

    def per_conversation(items_in):
        tokens_in, length_in, memory_in, conv_in = items_in
        projected, gate_raw = project(tokens_in[None], w_qkvz, w_beta_alpha)
        normed, final_memory, tail_rows = advance(projected, gate_raw, length_in[None], memory_in[None], conv_in[None], conv_weight, decay_log, step_bias, norm_gain)
        return (normed[0], final_memory[0], tail_rows[0])
    normed, final_memory, tail_rows = lax.map(per_conversation, (hidden, lengths, memories, conv_states))
    layer_out = jnp.dot(normed.reshape(-1, HV * DV), w_out, preferred_element_type=jnp.float32).astype(jnp.bfloat16)
    layer_out = layer_out.reshape(DIALOGUE_TOTAL, NEW, D)
    new_state_cache = state_cache.at[cache_index].set(final_memory)
    new_conv_cache = conv_cache.at[cache_index].set(tail_rows)
    return (layer_out, new_state_cache, new_conv_cache)
```

```python
import functools
import math

import jax
import jax.numpy as jnp
from jax import lax
from jax.experimental import pallas as pl
from jax.experimental.pallas import tpu as pltpu
from jax.sharding import PartitionSpec as P

F32, BF16 = jnp.float32, jnp.bfloat16
MESH = pl.DeviceIdType.MESH

NC = 16
NZ = 8
CONVS = 8
T = 128
DK = 128
CH = 512
SLOTS = 16
PAIR = 2


def mm(a, b, ca=1, cb=0):
    return lax.dot_general(
        a.astype(BF16), b.astype(BF16), (((ca,), (cb,)), ((), ())), preferred_element_type=F32
    )


def silu(v):
    return v * (0.5 * jnp.tanh(0.5 * v) + 0.5)


def kernel(
    hidden,
    lengths,
    owners,
    slots,
    state,
    conv_cache,
    w_qkvz,
    w_ba,
    conv_weight,
    decay_log,
    step_bias,
    norm_gain,
    w_out,
    layer_out,
    new_state,
    new_conv,
    convl,
    wbp,
    serve_slot,
    serve_live,
    cv_send,
    cv_recv,
    st_send,
    st_recv,
    ext,
    tail_tmp,
    wq,
    pk,
    u0,
    zg,
    eg_end,
    fin,
    nrm,
    rt_send,
    rt_recv,
    ybuf,
    cbuf,
    rsend,
    rrecv,
    newcf,
    cv_ss,
    cv_rs,
    st_ss,
    st_rs,
    rt_ss,
    rt_rs,
    co_ss,
    co_rs,
    ri_ss,
    ri_rs,
):
    me = lax.axis_index("cache")
    tt = lax.axis_index("tensor")
    z = tt // 2
    c = lax.rem(tt, 2)
    other = (me, z * 2 + 1 - c)
    up = (me, lax.rem(z + 1, NZ) * 2 + c)
    down = (me, lax.rem(z + NZ - 1, NZ) * 2 + c)

    barrier = pltpu.get_barrier_semaphore()

    def greet(d, carry):
        pl.semaphore_signal(barrier, inc=1, device_id=(lax.rem(me + d, NC), tt), device_id_type=MESH)
        return carry

    lax.fori_loop(1, NC, greet, 0)
    for peer in (other, up, down):
        pl.semaphore_signal(barrier, inc=1, device_id=peer, device_id_type=MESH)
    newcf[...] = conv_cache[...].astype(F32)
    convl[...] = jnp.zeros_like(convl)
    for s in range(SLOTS):
        for i in range(3):
            for b in range(4):
                convl[s, i * 4 + b : i * 4 + b + 1, :] = newcf[i, s : s + 1, b * 128 : (b + 1) * 128]
    wbp[...] = jnp.zeros_like(wbp)
    wbp[0:4, :] = w_ba[...].astype(F32)
    pl.semaphore_wait(barrier, NC - 1 + 3)

    def cv_copy(d):
        peer = lax.rem(me + d, NC)
        return pltpu.make_async_remote_copy(
            src_ref=cv_send.at[peer],
            dst_ref=cv_recv.at[me],
            send_sem=cv_ss.at[d],
            recv_sem=cv_rs.at[d],
            device_id=(peer, tt),
            device_id_type=MESH,
        )

    def st_copy(d):
        peer = lax.rem(me + d, NC)
        return pltpu.make_async_remote_copy(
            src_ref=st_send.at[peer],
            dst_ref=st_recv.at[me],
            send_sem=st_ss.at[d],
            recv_sem=st_rs.at[d],
            device_id=(peer, tt),
            device_id_type=MESH,
        )

    def conv_lane(peer):
        slot = jnp.int32(0)
        live = jnp.int32(0)
        for j in range(CONVS):
            hit = owners[peer * CONVS + j] == me
            slot = jnp.where(hit, slots[peer * CONVS + j], slot)
            live = jnp.where(hit, 1, live)
        serve_slot[peer] = slot
        serve_live[peer] = live
        return convl[slot].astype(BF16)

    tail_tmp[...] = jnp.zeros_like(tail_tmp)

    def send_conv(d, carry):
        peer = lax.rem(me + d, NC)
        cv_send[peer] = conv_lane(peer)
        cv_copy(d).start()
        return carry

    lax.fori_loop(1, NC, send_conv, 0)
    cv_recv[me] = conv_lane(me)

    def send_state(d, carry):
        peer = lax.rem(me + d, NC)
        st_send[peer] = state[serve_slot[peer]].astype(BF16)
        st_copy(d).start()
        return carry

    lax.fori_loop(1, NC, send_state, 0)
    st_recv[me] = state[serve_slot[me]].astype(BF16)

    def wait_conv(d, carry):
        cv_copy(d).wait()
        return carry

    lax.fori_loop(1, NC, wait_conv, 0)

    rows = lax.broadcasted_iota(jnp.int32, (T, T), 0)
    cols = lax.broadcasted_iota(jnp.int32, (T, T), 1)
    lane = lax.broadcasted_iota(jnp.int32, (1, T), 1)
    pos = lax.broadcasted_iota(jnp.int32, (T, 1), 0)

    def prepare(g, carry):
        x = hidden[pl.ds(g * PAIR, PAIR)].reshape(PAIR * T, hidden.shape[-1])
        projected = mm(x, w_qkvz[...]).astype(BF16)
        gates = mm(x, wbp[...], 1, 1).astype(BF16).astype(F32)
        rate = jnp.exp(
            jnp.where(lane == 2, decay_log[0], jnp.where(lane == 3, decay_log[1], 0.0))
        )
        bias = jnp.where(lane == 2, step_bias[0], jnp.where(lane == 3, step_bias[1], 0.0))
        inclusive = rows >= cols
        strictly = rows > cols
        tri = jnp.where(inclusive, 1.0, 0.0)
        chains = []
        for p in range(PAIR):
            j = g * PAIR + p
            length = lengths[me * CONVS + j]
            owner = owners[me * CONVS + j]
            live = pos < length
            mixed = projected[p * T : (p + 1) * T, :CH].astype(F32)
            z_part = projected[p * T : (p + 1) * T, CH:].astype(F32)
            held = cv_recv[owner].astype(F32)
            for i in range(3):
                for b in range(4):
                    ext[p, 5 + i : 6 + i, b * 128 : (b + 1) * 128] = held[i * 4 + b : i * 4 + b + 1, :]
            ext[p, 8 : 8 + T, :] = mixed
            convolved = conv_weight[3:4, :].astype(F32) * mixed
            for i in range(3):
                convolved = convolved + conv_weight[i : i + 1, :].astype(F32) * ext[p, 5 + i : 5 + i + T, :]
            for i in range(3):
                row = ext[p, pl.ds(5 + length + i, 1), :]
                for b in range(4):
                    tail_tmp[i * 4 + b : i * 4 + b + 1, :] = row[:, b * 128 : (b + 1) * 128]
            fin[j, 2 * DK : 2 * DK + 16, :] = tail_tmp[...].astype(BF16)
            act = silu(convolved)
            q = act[:, :DK]
            k = act[:, DK : 2 * DK]
            q = q * lax.rsqrt(jnp.sum(q * q, axis=-1, keepdims=True) + 1e-06) * (1.0 / math.sqrt(DK))
            k = k * lax.rsqrt(jnp.sum(k * k, axis=-1, keepdims=True) + 1e-06)
            zg[j] = jnp.where(
                live,
                silu(z_part) * jnp.concatenate([norm_gain[...], norm_gain[...]], axis=1),
                0.0,
            )
            raw = gates[p * T : (p + 1) * T, :]
            beta = jnp.where(live, 0.5 * jnp.tanh(0.5 * raw) + 0.5, 0.0)
            shifted = raw + bias
            decay = jnp.where(
                live,
                -rate * (jnp.maximum(shifted, 0.0) + jnp.log1p(jnp.exp(-jnp.abs(shifted)))),
                0.0,
            )
            total = jnp.dot(tri, decay, precision=lax.Precision.HIGHEST, preferred_element_type=F32)
            total_rows = total.T
            qk = mm(jnp.concatenate([k, q], axis=0), k, 1, 1)
            k_t = k.T
            for h in range(2):
                gc = total[:, 2 + h : 3 + h]
                gr = total_rows[2 + h : 3 + h, :]
                g_end = gr[:, T - 1 : T]
                bc = beta[:, h : h + 1]
                gap = jnp.where(inclusive, jnp.exp(jnp.where(inclusive, gc - gr, 0.0)), 0.0)
                lower = jnp.where(strictly, bc * qk[:T] * gap, 0.0)
                grow = jnp.exp(gc)
                wq[2 * j + h, T:, :] = (q * grow).astype(BF16)
                pk[2 * j + h, :T, :] = (qk[T:] * gap).astype(BF16)
                pk[2 * j + h, T:, :] = (k_t * jnp.exp(g_end - gr)).astype(BF16)
                eg_end[2 * j + h] = jnp.broadcast_to(jnp.exp(g_end), (8, T))
                right = jnp.concatenate(
                    [(bc * grow * k), bc * act[:, 2 * DK + h * T : 2 * DK + (h + 1) * T]], axis=1
                ).astype(BF16)
                chains.append((2 * j + h, lower, right))
        inverse = [
            jnp.where(rows == cols, 1.0, 0.0) - jnp.where(rows // 2 == cols // 2, low, 0.0)
            for _, low, _ in chains
        ]
        span = 2
        while span < T:
            block = (rows // (2 * span) == cols // (2 * span)) & (rows // span != cols // span)
            left = [mm(jnp.where(block, low, 0.0), inv) for (_, low, _), inv in zip(chains, inverse)]
            inverse = [inv - mm(inv, part) for inv, part in zip(inverse, left)]
            span *= 2
        for (at, _, right), inv in zip(chains, inverse):
            solved = mm(inv, right)
            wq[at, :T, :] = solved[:, :DK].astype(BF16)
            u0[at] = solved[:, DK:]
        return carry

    lax.fori_loop(0, CONVS // PAIR, prepare, 0)

    def wait_state(d, carry):
        st_copy(d).wait()
        return carry

    lax.fori_loop(1, NC, wait_state, 0)

    def finish(g, carry):
        for p in range(PAIR):
            j = g * PAIR + p
            owner = owners[me * CONVS + j]
            for h in range(2):
                at = 2 * j + h
                memory = st_recv[owner, h * DK : (h + 1) * DK, :]
                seen = mm(wq[at], memory)
                update = u0[at] - seen[:T]
                given = mm(pk[at], update)
                core = seen[T:] + given[:T]
                after = eg_end[at][0:1, :] * memory.astype(F32) + given[T:]
                fin[j, h * DK : (h + 1) * DK, :] = after.astype(BF16)
                scale = lax.rsqrt(jnp.mean(core * core, axis=-1, keepdims=True) + 1e-06)
                nrm[j, :, h * DK : (h + 1) * DK] = (
                    core * scale * zg[j, :, h * DK : (h + 1) * DK]
                ).astype(BF16)
        return carry

    lax.fori_loop(0, CONVS // PAIR, finish, 0)

    def rt_copy(d):
        peer = lax.rem(me + d, NC)
        return pltpu.make_async_remote_copy(
            src_ref=rt_send.at[peer],
            dst_ref=rt_recv.at[me],
            send_sem=rt_ss.at[d],
            recv_sem=rt_rs.at[d],
            device_id=(peer, tt),
            device_id_type=MESH,
        )

    def return_lane(peer):
        pick = jnp.int32(0)
        for j in range(CONVS):
            pick = jnp.where(owners[me * CONVS + j] == peer, j, pick)
        return fin[pick]

    def send_return(d, carry):
        peer = lax.rem(me + d, NC)
        rt_send[peer] = return_lane(peer)
        rt_copy(d).start()
        return carry

    lax.fori_loop(1, NC, send_return, 0)
    rt_recv[me] = return_lane(me)

    def core_copy(j):
        return pltpu.make_async_remote_copy(
            src_ref=ybuf.at[j, 1 - c],
            dst_ref=cbuf.at[j],
            send_sem=co_ss.at[j],
            recv_sem=co_rs.at[j],
            device_id=other,
            device_id_type=MESH,
        )

    def ring_copy(j, way, hop):
        if hop == 0:
            part = pl.ds(way * (T // 2), T // 2)
            src, dst = rsend.at[j, way, hop, part], rrecv.at[j, way, hop, part]
        else:
            src, dst = rsend.at[j, way, hop], rrecv.at[j, way, hop]
        return pltpu.make_async_remote_copy(
            src_ref=src,
            dst_ref=dst,
            send_sem=ri_ss.at[j, way, hop],
            recv_sem=ri_rs.at[j, way, hop],
            device_id=up if way == 0 else down,
            device_id_type=MESH,
        )

    def own_sum(j, dest):
        return ybuf[j, c, dest].astype(F32) + cbuf[j, dest].astype(F32)

    half = T // 2

    def turn(i, carry):
        @pl.when(i < CONVS)
        def _():
            normed = nrm[i]
            for n in range(NZ):
                y = mm(normed, w_out[:, n * 256 : (n + 1) * 256]).astype(BF16)
                ybuf[i, 0, n] = y[:, :128]
                ybuf[i, 1, n] = y[:, 128:]
            core_copy(i).start()

        @pl.when((i >= 1) & (i < CONVS + 1))
        def _():
            j = i - 1
            core_copy(j).wait()
            far = own_sum(j, lax.rem(z + 4, NZ)).astype(BF16)
            rsend[j, 0, 0, :half, :] = far[:half]
            rsend[j, 1, 0, half:, :] = far[half:]
            ring_copy(j, 0, 0).start()
            ring_copy(j, 1, 0).start()

        for hop in (1, 2, 3):

            @pl.when((i >= 1 + hop) & (i < CONVS + 1 + hop))
            def _(hop=hop):
                j = i - 1 - hop
                for way in (0, 1):
                    ring_copy(j, way, hop - 1).wait()
                    step = 4 - hop
                    dest = lax.rem(z + (step if way == 0 else NZ - step), NZ)
                    mine = own_sum(j, dest)
                    if hop == 1:
                        keep = slice(0, half) if way == 0 else slice(half, T)
                        alone = slice(half, T) if way == 0 else slice(0, half)
                        came = rrecv[j, way, 0, keep, :].astype(F32)
                        rsend[j, way, hop, keep, :] = (mine[keep] + came).astype(BF16)
                        rsend[j, way, hop, alone, :] = mine[alone].astype(BF16)
                    else:
                        came = rrecv[j, way, hop - 1].astype(F32)
                        rsend[j, way, hop] = (mine + came).astype(BF16)
                    ring_copy(j, way, hop).start()

        @pl.when(i >= 5)
        def _():
            j = i - 5
            ring_copy(j, 0, 3).wait()
            ring_copy(j, 1, 3).wait()
            total = own_sum(j, z) + rrecv[j, 0, 3].astype(F32) + rrecv[j, 1, 3].astype(F32)
            layer_out[j] = total.astype(BF16)

        return carry

    lax.fori_loop(0, CONVS + 5, turn, 0)

    def wait_return(d, carry):
        rt_copy(d).wait()
        return carry

    lax.fori_loop(1, NC, wait_return, 0)

    def store(s, carry):
        source = jnp.int32(0)
        found = jnp.int32(0)
        for d in range(NC):
            hit = (serve_slot[d] == s) & (serve_live[d] == 1)
            source = jnp.where(hit, d, source)
            found = jnp.where(hit, 1, found)
        came = rt_recv[source].astype(F32)
        fresh = found == 1
        new_state[s] = jnp.where(fresh, came[: 2 * DK], state[s])
        convl[s] = jnp.where(fresh, came[2 * DK :], convl[s])
        return carry

    lax.fori_loop(0, SLOTS, store, 0)
    for s in range(SLOTS):
        for i in range(3):
            for b in range(4):
                newcf[i, s : s + 1, b * 128 : (b + 1) * 128] = convl[s, i * 4 + b : i * 4 + b + 1, :]
    new_conv[...] = newcf[...].astype(BF16)


def local(
    hidden,
    lengths,
    owners,
    slot_ids,
    state_cache,
    conv_cache,
    w_qkvz,
    w_beta_alpha,
    conv_weight,
    decay_log,
    step_bias,
    norm_gain,
    w_out,
):
    vmem = pl.BlockSpec(memory_space=pltpu.VMEM)
    smem = pl.BlockSpec(memory_space=pltpu.SMEM)
    dma = pltpu.SemaphoreType.DMA
    layer_out, new_state, new_conv = pl.pallas_call(
        kernel,
        out_shape=(
            jax.ShapeDtypeStruct((CONVS, T, 128), BF16),
            jax.ShapeDtypeStruct((SLOTS, 2 * DK, T), F32),
            jax.ShapeDtypeStruct((3, SLOTS, CH), BF16),
        ),
        in_specs=[vmem, smem, smem, smem, vmem, vmem, vmem, vmem, vmem, smem, smem, vmem, vmem],
        out_specs=(vmem, vmem, vmem),
        scratch_shapes=[
            pltpu.VMEM((SLOTS, 16, 128), F32),
            pltpu.VMEM((128, 2048), F32),
            pltpu.SMEM((NC,), jnp.int32),
            pltpu.SMEM((NC,), jnp.int32),
            pltpu.VMEM((NC, 16, 128), BF16),
            pltpu.VMEM((NC, 16, 128), BF16),
            pltpu.VMEM((NC, 2 * DK, 128), BF16),
            pltpu.VMEM((NC, 2 * DK, 128), BF16),
            pltpu.VMEM((PAIR, 8 + T, CH), F32),
            pltpu.VMEM((16, 128), F32),
            pltpu.VMEM((2 * CONVS, 2 * T, DK), BF16),
            pltpu.VMEM((2 * CONVS, 2 * T, DK), BF16),
            pltpu.VMEM((2 * CONVS, T, DK), F32),
            pltpu.VMEM((CONVS, T, 2 * DK), F32),
            pltpu.VMEM((2 * CONVS, 8, 128), F32),
            pltpu.VMEM((CONVS, 2 * DK + 16, 128), BF16),
            pltpu.VMEM((CONVS, T, 2 * DK), BF16),
            pltpu.VMEM((NC, 2 * DK + 16, 128), BF16),
            pltpu.VMEM((NC, 2 * DK + 16, 128), BF16),
            pltpu.VMEM((CONVS, 2, NZ, T, 128), BF16),
            pltpu.VMEM((CONVS, NZ, T, 128), BF16),
            pltpu.VMEM((CONVS, 2, 4, T, 128), BF16),
            pltpu.VMEM((CONVS, 2, 4, T, 128), BF16),
            pltpu.VMEM((3, SLOTS, CH), F32),
            dma((NC,)),
            dma((NC,)),
            dma((NC,)),
            dma((NC,)),
            dma((NC,)),
            dma((NC,)),
            dma((CONVS,)),
            dma((CONVS,)),
            dma((CONVS, 2, 4)),
            dma((CONVS, 2, 4)),
        ],
        compiler_params=pltpu.CompilerParams(
            collective_id=0, has_side_effects=True, vmem_limit_bytes=56 * 1024 * 1024
        ),
    )(
        hidden,
        lengths,
        owners,
        slot_ids,
        state_cache.reshape(SLOTS, 2 * DK, 128),
        conv_cache.transpose(1, 2, 0, 3).reshape(3, SLOTS, CH),
        w_qkvz.reshape(2048, 768),
        w_beta_alpha.transpose(1, 2, 0).reshape(4, 2048),
        conv_weight.reshape(4, CH),
        decay_log,
        step_bias,
        norm_gain.reshape(1, 128),
        w_out,
    )
    return (
        layer_out,
        new_state.reshape(state_cache.shape),
        new_conv.reshape(3, 1, SLOTS, CH).transpose(2, 0, 1, 3),
    )


def solution(mesh):
    return jax.shard_map(
        local,
        mesh=mesh,
        in_specs=(
            P("cache", None, None),
            P(),
            P(),
            P(),
            P("cache", "tensor", None, None),
            P("cache", None, "tensor", None),
            P(None, "tensor", None),
            P(None, "tensor", None),
            P(None, "tensor", None),
            P("tensor"),
            P("tensor"),
            P(),
            P("tensor", None),
        ),
        out_specs=(
            P("cache", None, "tensor"),
            P("cache", "tensor", None, None),
            P("cache", None, "tensor", None),
        ),
        check_vma=False,
    )
```

```python
import functools
import math

import jax
import jax.numpy as jnp
from jax import lax
from jax.experimental import pallas as pl
from jax.experimental.pallas import tpu as pltpu
from jax.sharding import PartitionSpec as P

F32, BF16 = jnp.float32, jnp.bfloat16
MESH = pl.DeviceIdType.MESH

NC = 16
NZ = 8
CONVS = 8
T = 128
DK = 128
CH = 512
SLOTS = 16
PAIR = 2


def mm(a, b, ca=1, cb=0):
    return lax.dot_general(
        a.astype(BF16), b.astype(BF16), (((ca,), (cb,)), ((), ())), preferred_element_type=F32
    )


def silu(v):
    return v * (0.5 * jnp.tanh(0.5 * v) + 0.5)


def kernel(
    hidden_in,
    lengths,
    owners,
    slots,
    state_in,
    conv_cache,
    w_qkvz_in,
    w_ba,
    conv_weight,
    decay_log,
    step_bias,
    norm_gain,
    w_out_in,
    layer_out,
    new_state_out,
    new_conv,
    hidden,
    state,
    w_qkvz,
    w_out,
    new_state,
    in_s,
    out_s,
    convl,
    wbp,
    serve_slot,
    serve_live,
    cv_send,
    cv_recv,
    st_send,
    st_recv,
    ext,
    tail_tmp,
    wq,
    pk,
    u0,
    zg,
    eg_end,
    fin,
    nrm,
    rt_send,
    rt_recv,
    ybuf,
    cbuf,
    rsend,
    rrecv,
    newcf,
    cv_ss,
    cv_rs,
    st_ss,
    st_rs,
    rt_ss,
    rt_rs,
    co_ss,
    co_rs,
    ri_ss,
    ri_rs,
):
    me = lax.axis_index("cache")
    tt = lax.axis_index("tensor")
    z = tt // 2
    c = lax.rem(tt, 2)
    other = (me, z * 2 + 1 - c)
    up = (me, lax.rem(z + 1, NZ) * 2 + c)
    down = (me, lax.rem(z + NZ - 1, NZ) * 2 + c)

    loads = [
        pltpu.make_async_copy(src, dst, in_s.at[n])
        for n, (src, dst) in enumerate(
            [(state_in, state), (w_qkvz_in, w_qkvz), (hidden_in, hidden), (w_out_in, w_out)]
        )
    ]
    for load in loads:
        load.start()

    barrier = pltpu.get_barrier_semaphore()

    def greet(d, carry):
        pl.semaphore_signal(barrier, inc=1, device_id=(lax.rem(me + d, NC), tt), device_id_type=MESH)
        return carry

    lax.fori_loop(1, NC, greet, 0)
    for peer in (other, up, down):
        pl.semaphore_signal(barrier, inc=1, device_id=peer, device_id_type=MESH)
    newcf[...] = conv_cache[...].astype(F32)
    convl[...] = jnp.zeros_like(convl)
    for s in range(SLOTS):
        for i in range(3):
            for b in range(4):
                convl[s, i * 4 + b : i * 4 + b + 1, :] = newcf[i, s : s + 1, b * 128 : (b + 1) * 128]
    wbp[...] = jnp.zeros_like(wbp)
    wbp[0:4, :] = w_ba[...].astype(F32)
    pl.semaphore_wait(barrier, NC - 1 + 3)

    def cv_copy(d):
        peer = lax.rem(me + d, NC)
        return pltpu.make_async_remote_copy(
            src_ref=cv_send.at[peer],
            dst_ref=cv_recv.at[me],
            send_sem=cv_ss.at[d],
            recv_sem=cv_rs.at[d],
            device_id=(peer, tt),
            device_id_type=MESH,
        )

    def st_copy(d):
        peer = lax.rem(me + d, NC)
        return pltpu.make_async_remote_copy(
            src_ref=st_send.at[peer],
            dst_ref=st_recv.at[me],
            send_sem=st_ss.at[d],
            recv_sem=st_rs.at[d],
            device_id=(peer, tt),
            device_id_type=MESH,
        )

    def conv_lane(peer):
        slot = jnp.int32(0)
        live = jnp.int32(0)
        for j in range(CONVS):
            hit = owners[peer * CONVS + j] == me
            slot = jnp.where(hit, slots[peer * CONVS + j], slot)
            live = jnp.where(hit, 1, live)
        serve_slot[peer] = slot
        serve_live[peer] = live
        return convl[slot].astype(BF16)

    tail_tmp[...] = jnp.zeros_like(tail_tmp)

    def send_conv(d, carry):
        peer = lax.rem(me + d, NC)
        cv_send[peer] = conv_lane(peer)
        cv_copy(d).start()
        return carry

    lax.fori_loop(1, NC, send_conv, 0)
    cv_recv[me] = conv_lane(me)

    loads[0].wait()

    def pack_state(d, carry):
        peer = lax.rem(me + d, NC)
        st_send[peer] = state[serve_slot[peer]].astype(BF16)
        return carry

    lax.fori_loop(1, NC, pack_state, 0)
    st_recv[me] = state[serve_slot[me]].astype(BF16)

    def wait_conv(d, carry):
        cv_copy(d).wait()
        return carry

    lax.fori_loop(1, NC, wait_conv, 0)

    def send_state(d, carry):
        st_copy(d).start()
        return carry

    lax.fori_loop(1, NC, send_state, 0)
    loads[1].wait()
    loads[2].wait()

    rows = lax.broadcasted_iota(jnp.int32, (T, T), 0)
    cols = lax.broadcasted_iota(jnp.int32, (T, T), 1)
    lane = lax.broadcasted_iota(jnp.int32, (1, T), 1)
    pos = lax.broadcasted_iota(jnp.int32, (T, 1), 0)

    def prepare(g, carry):
        x = hidden[pl.ds(g * PAIR, PAIR)].reshape(PAIR * T, hidden.shape[-1])
        projected = mm(x, w_qkvz[...]).astype(BF16)
        gates = mm(x, wbp[...], 1, 1).astype(BF16).astype(F32)
        rate = jnp.exp(
            jnp.where(lane == 2, decay_log[0], jnp.where(lane == 3, decay_log[1], 0.0))
        )
        bias = jnp.where(lane == 2, step_bias[0], jnp.where(lane == 3, step_bias[1], 0.0))
        inclusive = rows >= cols
        strictly = rows > cols
        tri = jnp.where(inclusive, 1.0, 0.0)
        chains = []
        for p in range(PAIR):
            j = g * PAIR + p
            length = lengths[me * CONVS + j]
            owner = owners[me * CONVS + j]
            live = pos < length
            mixed = projected[p * T : (p + 1) * T, :CH].astype(F32)
            z_part = projected[p * T : (p + 1) * T, CH:].astype(F32)
            held = cv_recv[owner].astype(F32)
            for i in range(3):
                for b in range(4):
                    ext[p, 5 + i : 6 + i, b * 128 : (b + 1) * 128] = held[i * 4 + b : i * 4 + b + 1, :]
            ext[p, 8 : 8 + T, :] = mixed
            convolved = conv_weight[3:4, :].astype(F32) * mixed
            for i in range(3):
                convolved = convolved + conv_weight[i : i + 1, :].astype(F32) * ext[p, 5 + i : 5 + i + T, :]
            for i in range(3):
                row = ext[p, pl.ds(5 + length + i, 1), :]
                for b in range(4):
                    tail_tmp[i * 4 + b : i * 4 + b + 1, :] = row[:, b * 128 : (b + 1) * 128]
            fin[j, 2 * DK : 2 * DK + 16, :] = tail_tmp[...].astype(BF16)
            act = silu(convolved)
            q = act[:, :DK]
            k = act[:, DK : 2 * DK]
            q = q * lax.rsqrt(jnp.sum(q * q, axis=-1, keepdims=True) + 1e-06) * (1.0 / math.sqrt(DK))
            k = k * lax.rsqrt(jnp.sum(k * k, axis=-1, keepdims=True) + 1e-06)
            zg[j] = jnp.where(
                live,
                silu(z_part) * jnp.concatenate([norm_gain[...], norm_gain[...]], axis=1),
                0.0,
            )
            raw = gates[p * T : (p + 1) * T, :]
            beta = jnp.where(live, 0.5 * jnp.tanh(0.5 * raw) + 0.5, 0.0)
            shifted = raw + bias
            decay = jnp.where(
                live,
                -rate * (jnp.maximum(shifted, 0.0) + jnp.log1p(jnp.exp(-jnp.abs(shifted)))),
                0.0,
            )
            total = jnp.dot(tri, decay, precision=lax.Precision.HIGHEST, preferred_element_type=F32)
            total_rows = total.T
            qk = mm(jnp.concatenate([k, q], axis=0), k, 1, 1)
            k_t = k.T
            for h in range(2):
                gc = total[:, 2 + h : 3 + h]
                gr = total_rows[2 + h : 3 + h, :]
                g_end = gr[:, T - 1 : T]
                bc = beta[:, h : h + 1]
                gap = jnp.where(inclusive, jnp.exp(jnp.where(inclusive, gc - gr, 0.0)), 0.0)
                lower = jnp.where(strictly, bc * qk[:T] * gap, 0.0)
                grow = jnp.exp(gc)
                wq[2 * j + h, T:, :] = (q * grow).astype(BF16)
                pk[2 * j + h, :T, :] = (qk[T:] * gap).astype(BF16)
                pk[2 * j + h, T:, :] = (k_t * jnp.exp(g_end - gr)).astype(BF16)
                eg_end[2 * j + h] = jnp.broadcast_to(jnp.exp(g_end), (8, T))
                right = jnp.concatenate(
                    [(bc * grow * k), bc * act[:, 2 * DK + h * T : 2 * DK + (h + 1) * T]], axis=1
                ).astype(BF16)
                chains.append((2 * j + h, lower, right))
        inverse = [
            jnp.where(rows == cols, 1.0, 0.0) - jnp.where(rows // 2 == cols // 2, low, 0.0)
            for _, low, _ in chains
        ]
        span = 2
        while span < T:
            block = (rows // (2 * span) == cols // (2 * span)) & (rows // span != cols // span)
            left = [mm(jnp.where(block, low, 0.0), inv) for (_, low, _), inv in zip(chains, inverse)]
            inverse = [inv - mm(inv, part) for inv, part in zip(inverse, left)]
            span *= 2
        for (at, _, right), inv in zip(chains, inverse):
            solved = mm(inv, right)
            wq[at, :T, :] = solved[:, :DK].astype(BF16)
            u0[at] = solved[:, DK:]
        return carry

    lax.fori_loop(0, CONVS // PAIR, prepare, 0)

    def wait_state(d, carry):
        st_copy(d).wait()
        return carry

    lax.fori_loop(1, NC, wait_state, 0)

    def finish(g, carry):
        for p in range(PAIR):
            j = g * PAIR + p
            owner = owners[me * CONVS + j]
            for h in range(2):
                at = 2 * j + h
                memory = st_recv[owner, h * DK : (h + 1) * DK, :]
                seen = mm(wq[at], memory)
                update = u0[at] - seen[:T]
                given = mm(pk[at], update)
                core = seen[T:] + given[:T]
                after = eg_end[at][0:1, :] * memory.astype(F32) + given[T:]
                fin[j, h * DK : (h + 1) * DK, :] = after.astype(BF16)
                scale = lax.rsqrt(jnp.mean(core * core, axis=-1, keepdims=True) + 1e-06)
                nrm[j, :, h * DK : (h + 1) * DK] = (
                    core * scale * zg[j, :, h * DK : (h + 1) * DK]
                ).astype(BF16)
        return carry

    def rt_copy(d):
        peer = lax.rem(me + d, NC)
        return pltpu.make_async_remote_copy(
            src_ref=rt_send.at[peer],
            dst_ref=rt_recv.at[me],
            send_sem=rt_ss.at[d],
            recv_sem=rt_rs.at[d],
            device_id=(peer, tt),
            device_id_type=MESH,
        )

    def return_lane(peer):
        pick = jnp.int32(0)
        for j in range(CONVS):
            pick = jnp.where(owners[me * CONVS + j] == peer, j, pick)
        return fin[pick]

    def send_return(d, carry):
        peer = lax.rem(me + d, NC)
        rt_send[peer] = return_lane(peer)
        rt_copy(d).start()
        return carry

    def core_copy(j):
        return pltpu.make_async_remote_copy(
            src_ref=ybuf.at[j, 1 - c],
            dst_ref=cbuf.at[j],
            send_sem=co_ss.at[j],
            recv_sem=co_rs.at[j],
            device_id=other,
            device_id_type=MESH,
        )

    def ring_copy(j, way, hop):
        if hop == 0:
            part = pl.ds(way * (T // 2), T // 2)
            src, dst = rsend.at[j, way, hop, part], rrecv.at[j, way, hop, part]
        else:
            src, dst = rsend.at[j, way, hop], rrecv.at[j, way, hop]
        return pltpu.make_async_remote_copy(
            src_ref=src,
            dst_ref=dst,
            send_sem=ri_ss.at[j, way, hop],
            recv_sem=ri_rs.at[j, way, hop],
            device_id=up if way == 0 else down,
            device_id_type=MESH,
        )

    def own_sum(j, dest):
        return ybuf[j, c, dest].astype(F32) + cbuf[j, dest].astype(F32)

    half = T // 2

    def far_hop(j):
        core_copy(j).wait()
        far = own_sum(j, lax.rem(z + 4, NZ)).astype(BF16)
        rsend[j, 0, 0, :half, :] = far[:half]
        rsend[j, 1, 0, half:, :] = far[half:]
        ring_copy(j, 0, 0).start()
        ring_copy(j, 1, 0).start()

    def next_hop(j, hop):
        for way in (0, 1):
            ring_copy(j, way, hop - 1).wait()
            step = 4 - hop
            dest = lax.rem(z + (step if way == 0 else NZ - step), NZ)
            mine = own_sum(j, dest)
            if hop == 1:
                keep = slice(0, half) if way == 0 else slice(half, T)
                alone = slice(half, T) if way == 0 else slice(0, half)
                came = rrecv[j, way, 0, keep, :].astype(F32)
                rsend[j, way, hop, keep, :] = (mine[keep] + came).astype(BF16)
                rsend[j, way, hop, alone, :] = mine[alone].astype(BF16)
            else:
                came = rrecv[j, way, hop - 1].astype(F32)
                rsend[j, way, hop] = (mine + came).astype(BF16)
            ring_copy(j, way, hop).start()

    def turn(i, carry):
        @pl.when(i < CONVS // PAIR)
        def _():
            finish(i, 0)

        @pl.when(i < CONVS)
        def _():
            normed = nrm[i]
            for n in range(NZ):
                y = mm(normed, w_out[:, n * 256 : (n + 1) * 256]).astype(BF16)
                ybuf[i, 0, n] = y[:, :128]
                ybuf[i, 1, n] = y[:, 128:]
            core_copy(i).start()

        @pl.when(i >= 1)
        def _():
            far_hop(i - 1)

        @pl.when(i >= 3)
        def _():
            next_hop(i - 3, 1)

        return carry

    loads[3].wait()
    lax.fori_loop(0, CONVS // PAIR, turn, 0)
    lax.fori_loop(1, NC, send_return, 0)
    rt_recv[me] = return_lane(me)
    lax.fori_loop(CONVS // PAIR, CONVS + 1, turn, 0)
    for hop, first in ((1, CONVS - 2), (2, 0), (3, 0)):

        def hops(j, carry, hop=hop):
            next_hop(j, hop)
            return carry

        lax.fori_loop(first, CONVS, hops, 0)

    def wait_return(d, carry):
        rt_copy(d).wait()
        return carry

    lax.fori_loop(1, NC, wait_return, 0)

    def leave(s):
        return pltpu.make_async_copy(new_state.at[s], new_state_out.at[s], out_s.at[s])

    def store(s, carry):
        source = jnp.int32(0)
        found = jnp.int32(0)
        for d in range(NC):
            hit = (serve_slot[d] == s) & (serve_live[d] == 1)
            source = jnp.where(hit, d, source)
            found = jnp.where(hit, 1, found)
        came = rt_recv[source].astype(F32)
        fresh = found == 1
        new_state[s] = jnp.where(fresh, came[: 2 * DK], state[s])
        convl[s] = jnp.where(fresh, came[2 * DK :], convl[s])
        leave(s).start()
        return carry

    lax.fori_loop(0, SLOTS, store, 0)
    for s in range(SLOTS):
        for i in range(3):
            for b in range(4):
                newcf[i, s : s + 1, b * 128 : (b + 1) * 128] = convl[s, i * 4 + b : i * 4 + b + 1, :]
    new_conv[...] = newcf[...].astype(BF16)

    def last(j, carry):
        ring_copy(j, 0, 3).wait()
        ring_copy(j, 1, 3).wait()
        total = own_sum(j, z) + rrecv[j, 0, 3].astype(F32) + rrecv[j, 1, 3].astype(F32)
        layer_out[j] = total.astype(BF16)
        return carry

    lax.fori_loop(0, CONVS, last, 0)

    def left(s, carry):
        leave(s).wait()
        return carry

    lax.fori_loop(0, SLOTS, left, 0)


def hand_on(layer_in, state_in, conv_in, layer_out, state_out, conv_out, layer, state, conv, came, gone):
    parts = [(layer_in, layer, layer_out), (conv_in, conv, conv_out)]
    for n in range(8):
        part = pl.ds(2 * n, 2)
        parts.append((state_in.at[part], state.at[part], state_out.at[part]))
    take = [pltpu.make_async_copy(a, b, came.at[n]) for n, (a, b, _) in enumerate(parts)]
    give = [pltpu.make_async_copy(b, c, gone.at[n]) for n, (_, b, c) in enumerate(parts)]
    for copy in take:
        copy.start()
    for here, there in zip(take, give):
        here.wait()
        there.start()
    for copy in give:
        copy.wait()


def local(
    hidden,
    lengths,
    owners,
    slot_ids,
    state_cache,
    conv_cache,
    w_qkvz,
    w_beta_alpha,
    conv_weight,
    decay_log,
    step_bias,
    norm_gain,
    w_out,
):
    vmem = pl.BlockSpec(memory_space=pltpu.VMEM)
    smem = pl.BlockSpec(memory_space=pltpu.SMEM)
    dma = pltpu.SemaphoreType.DMA
    far = pl.BlockSpec(memory_space=pl.ANY)
    hbm = pl.BlockSpec(memory_space=pltpu.HBM)
    results = (
        jax.ShapeDtypeStruct((CONVS, T, 128), BF16),
        jax.ShapeDtypeStruct((SLOTS, 2 * DK, T), F32),
        jax.ShapeDtypeStruct((3, SLOTS, CH), BF16),
    )
    worked = pl.pallas_call(
        kernel,
        out_shape=results,
        in_specs=[far, smem, smem, smem, far, vmem, far, vmem, vmem, smem, smem, vmem, far],
        out_specs=(vmem, far, vmem),
        scratch_shapes=[
            pltpu.VMEM((CONVS, T, 2048), BF16),
            pltpu.VMEM((SLOTS, 2 * DK, 128), F32),
            pltpu.VMEM((2048, 768), BF16),
            pltpu.VMEM((256, 2048), BF16),
            pltpu.VMEM((SLOTS, 2 * DK, 128), F32),
            dma((4,)),
            dma((SLOTS,)),
            pltpu.VMEM((SLOTS, 16, 128), F32),
            pltpu.VMEM((128, 2048), F32),
            pltpu.SMEM((NC,), jnp.int32),
            pltpu.SMEM((NC,), jnp.int32),
            pltpu.VMEM((NC, 16, 128), BF16),
            pltpu.VMEM((NC, 16, 128), BF16),
            pltpu.VMEM((NC, 2 * DK, 128), BF16),
            pltpu.VMEM((NC, 2 * DK, 128), BF16),
            pltpu.VMEM((PAIR, 8 + T, CH), F32),
            pltpu.VMEM((16, 128), F32),
            pltpu.VMEM((2 * CONVS, 2 * T, DK), BF16),
            pltpu.VMEM((2 * CONVS, 2 * T, DK), BF16),
            pltpu.VMEM((2 * CONVS, T, DK), F32),
            pltpu.VMEM((CONVS, T, 2 * DK), F32),
            pltpu.VMEM((2 * CONVS, 8, 128), F32),
            pltpu.VMEM((CONVS, 2 * DK + 16, 128), BF16),
            pltpu.VMEM((CONVS, T, 2 * DK), BF16),
            pltpu.VMEM((NC, 2 * DK + 16, 128), BF16),
            pltpu.VMEM((NC, 2 * DK + 16, 128), BF16),
            pltpu.VMEM((CONVS, 2, NZ, T, 128), BF16),
            pltpu.VMEM((CONVS, NZ, T, 128), BF16),
            pltpu.VMEM((CONVS, 2, 4, T, 128), BF16),
            pltpu.VMEM((CONVS, 2, 4, T, 128), BF16),
            pltpu.VMEM((3, SLOTS, CH), F32),
            dma((NC,)),
            dma((NC,)),
            dma((NC,)),
            dma((NC,)),
            dma((NC,)),
            dma((NC,)),
            dma((CONVS,)),
            dma((CONVS,)),
            dma((CONVS, 2, 4)),
            dma((CONVS, 2, 4)),
        ],
        compiler_params=pltpu.CompilerParams(
            collective_id=0, has_side_effects=True, vmem_limit_bytes=56 * 1024 * 1024
        ),
    )(
        hidden,
        lengths,
        owners,
        slot_ids,
        state_cache.reshape(SLOTS, 2 * DK, 128),
        conv_cache.transpose(1, 2, 0, 3).reshape(3, SLOTS, CH),
        w_qkvz.reshape(2048, 768),
        w_beta_alpha.transpose(1, 2, 0).reshape(4, 2048),
        conv_weight.reshape(4, CH),
        decay_log,
        step_bias,
        norm_gain.reshape(1, 128),
        w_out,
    )
    layer_out, new_state, new_conv = pl.pallas_call(
        hand_on,
        out_shape=results,
        in_specs=[hbm, hbm, hbm],
        out_specs=(hbm, hbm, hbm),
        scratch_shapes=[pltpu.VMEM(r.shape, r.dtype) for r in results] + [dma((10,)), dma((10,))],
    )(*worked)
    return (
        layer_out,
        new_state.reshape(state_cache.shape),
        new_conv.reshape(3, 1, SLOTS, CH).transpose(2, 0, 1, 3),
    )


def solution(mesh):
    return jax.shard_map(
        local,
        mesh=mesh,
        in_specs=(
            P("cache", None, None),
            P(),
            P(),
            P(),
            P("cache", "tensor", None, None),
            P("cache", None, "tensor", None),
            P(None, "tensor", None),
            P(None, "tensor", None),
            P(None, "tensor", None),
            P("tensor"),
            P("tensor"),
            P(),
            P("tensor", None),
        ),
        out_specs=(
            P("cache", None, "tensor"),
            P("cache", "tensor", None, None),
            P("cache", None, "tensor", None),
        ),
        check_vma=False,
    )
```

```python
import functools
import math

import jax
import jax.numpy as jnp
from jax import lax
from jax.experimental import pallas as pl
from jax.experimental.pallas import tpu as pltpu
from jax.sharding import PartitionSpec as P

F32, BF16 = jnp.float32, jnp.bfloat16
MESH = pl.DeviceIdType.MESH

NC = 16
NZ = 8
CONVS = 8
T = 128
DK = 128
CH = 512
SLOTS = 16
PAIR = 2
STEP = 2
PREP = 4
ORDER = sorted(range(1, NC), key=lambda n: -(min(n // 4, 4 - n // 4) + min(n % 4, 4 - n % 4)))


def mm(a, b, ca=1, cb=0):
    return lax.dot_general(
        a.astype(BF16), b.astype(BF16), (((ca,), (cb,)), ((), ())), preferred_element_type=F32
    )


def silu(v):
    return v * (0.5 * jnp.tanh(0.5 * v) + 0.5)


def kernel(
    hidden_in,
    lengths,
    owners,
    slots,
    state_in,
    conv_cache,
    w_qkvz_in,
    w_ba,
    conv_weight,
    decay_log,
    step_bias,
    norm_gain,
    w_out_in,
    layer_out,
    new_state_out,
    new_conv,
    hidden,
    state,
    w_qkvz,
    w_out,
    new_state,
    in_s,
    out_s,
    convl,
    wbp,
    proj,
    gate,
    serve_slot,
    serve_live,
    cv_send,
    cv_recv,
    st_send,
    st_recv,
    ext,
    tail_tmp,
    wq,
    pk,
    u0,
    zg,
    eg_end,
    fin,
    nrm,
    rt_send,
    rt_recv,
    nrm_other,
    w_pair,
    ybuf,
    rsend,
    rrecv,
    newcf,
    cv_ss,
    cv_rs,
    st_ss,
    st_rs,
    rt_ss,
    rt_rs,
    nx_ss,
    nx_rs,
    co_ss,
    co_rs,
    ri_ss,
    ri_rs,
):
    me = lax.axis_index("cache")
    tt = lax.axis_index("tensor")
    z = tt // 2
    c = lax.rem(tt, 2)
    other = (me, z * 2 + 1 - c)
    up = (me, lax.rem(z + 1, NZ) * 2 + c)
    down = (me, lax.rem(z + NZ - 1, NZ) * 2 + c)

    def ahead(n):
        return lax.rem(me // 4 + n // 4, 4) * 4 + lax.rem(lax.rem(me, 4) + lax.rem(n, 4), 4)

    loads = [
        pltpu.make_async_copy(src, dst, in_s.at[n])
        for n, (src, dst) in enumerate(
            [(state_in, state), (w_out_in, w_out), (w_qkvz_in, w_qkvz), (hidden_in, hidden)]
        )
    ]
    for load in loads:
        load.start()

    barrier = pltpu.get_barrier_semaphore()

    def greet(d, carry):
        pl.semaphore_signal(barrier, inc=1, device_id=(ahead(d), tt), device_id_type=MESH)
        return carry

    lax.fori_loop(1, NC, greet, 0)
    for peer in (other, up, down):
        pl.semaphore_signal(barrier, inc=1, device_id=peer, device_id_type=MESH)
    newcf[...] = conv_cache[...].astype(F32)
    convl[...] = jnp.zeros_like(convl)
    for s in range(SLOTS):
        for i in range(3):
            for b in range(4):
                convl[s, i * 4 + b : i * 4 + b + 1, :] = newcf[i, s : s + 1, b * 128 : (b + 1) * 128]
    pl.semaphore_wait(barrier, NC - 1 + 3)

    def cv_copy(d):
        peer = ahead(d)
        return pltpu.make_async_remote_copy(
            src_ref=cv_send.at[peer],
            dst_ref=cv_recv.at[me],
            send_sem=cv_ss.at[d],
            recv_sem=cv_rs.at[d],
            device_id=(peer, tt),
            device_id_type=MESH,
        )

    def st_copy(d):
        peer = ahead(d)
        return pltpu.make_async_remote_copy(
            src_ref=st_send.at[peer],
            dst_ref=st_recv.at[me],
            send_sem=st_ss.at[d],
            recv_sem=st_rs.at[d],
            device_id=(peer, tt),
            device_id_type=MESH,
        )

    def conv_lane(peer):
        slot = jnp.int32(0)
        live = jnp.int32(0)
        for j in range(CONVS):
            hit = owners[peer * CONVS + j] == me
            slot = jnp.where(hit, slots[peer * CONVS + j], slot)
            live = jnp.where(hit, 1, live)
        serve_slot[peer] = slot
        serve_live[peer] = live
        return convl[slot].astype(BF16)

    tail_tmp[...] = jnp.zeros_like(tail_tmp)

    def send_conv(d, carry):
        peer = ahead(d)
        cv_send[peer] = conv_lane(peer)
        cv_copy(d).start()
        return carry

    lax.fori_loop(1, NC, send_conv, 0)
    cv_recv[me] = conv_lane(me)

    loads[0].wait()

    for d in ORDER:
        peer = ahead(d)
        st_send[peer] = state[serve_slot[peer]].astype(BF16)
    st_recv[me] = state[serve_slot[me]].astype(BF16)

    def columns(r, core):
        return pl.ds(pl.multiple_of((lax.rem(z + 4 + r, NZ) * 2 + core) * 128, 128), 128)

    def weight_copy(r):
        return pltpu.make_async_remote_copy(
            src_ref=w_out.at[:, columns(r, 1 - c)],
            dst_ref=w_pair.at[pl.ds(256, 256), pl.ds(r * 128, 128)],
            send_sem=co_ss.at[r],
            recv_sem=co_rs.at[r],
            device_id=other,
            device_id_type=MESH,
        )

    loads[1].wait()
    for r in range(NZ):
        weight_copy(r).start()
    for r in range(NZ):
        w_pair[0:256, r * 128 : (r + 1) * 128] = w_out[:, columns(r, c)]

    def wait_conv(d, carry):
        cv_copy(d).wait()
        return carry

    lax.fori_loop(1, NC, wait_conv, 0)

    for d in ORDER:
        st_copy(d).start()

    wbp[...] = jnp.zeros_like(wbp)
    wbp[0:4, :] = w_ba[...].astype(F32)
    loads[2].wait()
    loads[3].wait()

    def project(g, carry):
        x = hidden[pl.ds(g * STEP, STEP)].reshape(STEP * T, hidden.shape[-1])
        projected = mm(x, w_qkvz[...]).astype(BF16)
        gates = mm(x, wbp[...], 1, 1).astype(BF16).astype(F32)
        for p in range(STEP):
            proj[g * STEP + p] = projected[p * T : (p + 1) * T]
            gate[g * STEP + p] = gates[p * T : (p + 1) * T]
        return carry

    lax.fori_loop(0, CONVS // STEP, project, 0)

    rows = lax.broadcasted_iota(jnp.int32, (T, T), 0)
    cols = lax.broadcasted_iota(jnp.int32, (T, T), 1)
    lane = lax.broadcasted_iota(jnp.int32, (1, T), 1)
    pos = lax.broadcasted_iota(jnp.int32, (T, 1), 0)

    def prepare(g, carry):
        rate = jnp.exp(
            jnp.where(lane == 2, decay_log[0], jnp.where(lane == 3, decay_log[1], 0.0))
        )
        bias = jnp.where(lane == 2, step_bias[0], jnp.where(lane == 3, step_bias[1], 0.0))
        inclusive = rows >= cols
        strictly = rows > cols
        tri = jnp.where(inclusive, 1.0, 0.0)
        chains = []
        for p in range(PREP):
            j = g * PREP + p
            length = lengths[me * CONVS + j]
            owner = owners[me * CONVS + j]
            live = pos < length
            mixed = proj[j, :, :CH].astype(F32)
            z_part = proj[j, :, CH:].astype(F32)
            held = cv_recv[owner].astype(F32)
            for i in range(3):
                for b in range(4):
                    ext[p, 5 + i : 6 + i, b * 128 : (b + 1) * 128] = held[i * 4 + b : i * 4 + b + 1, :]
            ext[p, 8 : 8 + T, :] = mixed
            convolved = conv_weight[3:4, :].astype(F32) * mixed
            for i in range(3):
                convolved = convolved + conv_weight[i : i + 1, :].astype(F32) * ext[p, 5 + i : 5 + i + T, :]
            for i in range(3):
                row = ext[p, pl.ds(5 + length + i, 1), :]
                for b in range(4):
                    tail_tmp[p, i * 4 + b : i * 4 + b + 1, :] = row[:, b * 128 : (b + 1) * 128]
            fin[j, 2 * DK : 2 * DK + 16, :] = tail_tmp[p].astype(BF16)
            act = silu(convolved)
            q = act[:, :DK]
            k = act[:, DK : 2 * DK]
            q = q * lax.rsqrt(jnp.sum(q * q, axis=-1, keepdims=True) + 1e-06) * (1.0 / math.sqrt(DK))
            k = k * lax.rsqrt(jnp.sum(k * k, axis=-1, keepdims=True) + 1e-06)
            zg[j] = jnp.where(
                live,
                silu(z_part) * jnp.concatenate([norm_gain[...], norm_gain[...]], axis=1),
                0.0,
            )
            raw = gate[j]
            beta = jnp.where(live, 0.5 * jnp.tanh(0.5 * raw) + 0.5, 0.0)
            shifted = raw + bias
            decay = jnp.where(
                live,
                -rate * (jnp.maximum(shifted, 0.0) + jnp.log1p(jnp.exp(-jnp.abs(shifted)))),
                0.0,
            )
            total = jnp.dot(tri, decay, precision=lax.Precision.HIGHEST, preferred_element_type=F32)
            total_rows = total.T
            qk = mm(jnp.concatenate([k, q], axis=0), k, 1, 1)
            k_t = k.T
            for h in range(2):
                gc = total[:, 2 + h : 3 + h]
                gr = total_rows[2 + h : 3 + h, :]
                g_end = gr[:, T - 1 : T]
                bc = beta[:, h : h + 1]
                gap = jnp.where(inclusive, jnp.exp(jnp.where(inclusive, gc - gr, 0.0)), 0.0)
                lower = jnp.where(strictly, bc * qk[:T] * gap, 0.0)
                grow = jnp.exp(gc)
                wq[2 * j + h, T:, :] = (q * grow).astype(BF16)
                pk[2 * j + h, :T, :] = (qk[T:] * gap).astype(BF16)
                pk[2 * j + h, T:, :] = (k_t * jnp.exp(g_end - gr)).astype(BF16)
                eg_end[2 * j + h] = jnp.broadcast_to(jnp.exp(g_end), (8, T))
                right = jnp.concatenate(
                    [(bc * grow * k), bc * act[:, 2 * DK + h * T : 2 * DK + (h + 1) * T]], axis=1
                ).astype(BF16)
                chains.append((2 * j + h, lower, right))
        inverse = [
            jnp.where(rows == cols, 1.0, 0.0) - jnp.where(rows // 2 == cols // 2, low, 0.0)
            for _, low, _ in chains
        ]
        span = 2
        while span < T:
            block = (rows // (4 * span) == cols // (4 * span)) & (rows // span != cols // span)
            nil = [mm(inv, jnp.where(block, low, 0.0)) for (_, low, _), inv in zip(chains, inverse)]
            square = [mm(n, n) for n in nil]
            first = [inv - mm(n, inv) for n, inv in zip(nil, inverse)]
            inverse = [f + mm(q, f) for q, f in zip(square, first)]
            span *= 4
        for (at, _, right), inv in zip(chains, inverse):
            solved = mm(inv, right)
            wq[at, :T, :] = solved[:, :DK].astype(BF16)
            u0[at] = solved[:, DK:]
        return carry

    lax.fori_loop(0, CONVS // PREP, prepare, 0)

    def wait_state(d, carry):
        st_copy(d).wait()
        return carry

    lax.fori_loop(1, NC, wait_state, 0)

    def finish(g, carry):
        for p in range(PAIR):
            j = g * PAIR + p
            owner = owners[me * CONVS + j]
            for h in range(2):
                at = 2 * j + h
                memory = st_recv[owner, h * DK : (h + 1) * DK, :]
                seen = mm(wq[at], memory)
                update = u0[at] - seen[:T]
                given = mm(pk[at], update)
                core = seen[T:] + given[:T]
                after = eg_end[at][0:1, :] * memory.astype(F32) + given[T:]
                fin[j, h * DK : (h + 1) * DK, :] = after.astype(BF16)
                scale = lax.rsqrt(jnp.mean(core * core, axis=-1, keepdims=True) + 1e-06)
                nrm[j, :, h * DK : (h + 1) * DK] = (
                    core * scale * zg[j, :, h * DK : (h + 1) * DK]
                ).astype(BF16)
        return carry

    def rt_copy(d):
        peer = ahead(d)
        return pltpu.make_async_remote_copy(
            src_ref=rt_send.at[peer],
            dst_ref=rt_recv.at[me],
            send_sem=rt_ss.at[d],
            recv_sem=rt_rs.at[d],
            device_id=(peer, tt),
            device_id_type=MESH,
        )

    def return_lane(peer):
        pick = jnp.int32(0)
        for j in range(CONVS):
            pick = jnp.where(owners[me * CONVS + j] == peer, j, pick)
        return fin[pick]

    def send_return(d, carry):
        peer = ahead(d)
        rt_send[peer] = return_lane(peer)
        rt_copy(d).start()
        return carry

    def norm_copy(g):
        pair = pl.ds(g * PAIR, PAIR)
        return pltpu.make_async_remote_copy(
            src_ref=nrm.at[pair],
            dst_ref=nrm_other.at[pair],
            send_sem=nx_ss.at[g],
            recv_sem=nx_rs.at[g],
            device_id=other,
            device_id_type=MESH,
        )

    def ring_copy(j, way, hop):
        if hop == 0:
            part = pl.ds(way * (T // 2), T // 2)
            src, dst = rsend.at[j, way, hop, part], rrecv.at[j, way, hop, part]
        else:
            src, dst = rsend.at[j, way, hop], rrecv.at[j, way, hop]
        return pltpu.make_async_remote_copy(
            src_ref=src,
            dst_ref=dst,
            send_sem=ri_ss.at[j, way, hop],
            recv_sem=ri_rs.at[j, way, hop],
            device_id=up if way == 0 else down,
            device_id_type=MESH,
        )

    half = T // 2

    def far_hop(j):
        far = ybuf[j, 0].astype(BF16)
        rsend[j, 0, 0, :half, :] = far[:half]
        rsend[j, 1, 0, half:, :] = far[half:]
        ring_copy(j, 0, 0).start()
        ring_copy(j, 1, 0).start()

    def next_hop(j, hop):
        for way in (0, 1):
            ring_copy(j, way, hop - 1).wait()
            mine = ybuf[j, NZ - hop if way == 0 else hop]
            if hop == 1:
                keep = slice(0, half) if way == 0 else slice(half, T)
                alone = slice(half, T) if way == 0 else slice(0, half)
                came = rrecv[j, way, 0, keep, :].astype(F32)
                rsend[j, way, hop, keep, :] = (mine[keep] + came).astype(BF16)
                rsend[j, way, hop, alone, :] = mine[alone].astype(BF16)
            else:
                came = rrecv[j, way, hop - 1].astype(F32)
                rsend[j, way, hop] = (mine + came).astype(BF16)
            ring_copy(j, way, hop).start()

    def begin(g):
        finish(g, 0)
        norm_copy(g).start()

    def out(g):
        norm_copy(g).wait()
        pair = pl.ds(g * PAIR, PAIR)
        x = jnp.concatenate([nrm[pair].reshape(PAIR * T, 256), nrm_other[pair].reshape(PAIR * T, 256)], axis=1)
        for n in range(NZ // 2):
            y = mm(x, w_pair[:, n * 256 : (n + 1) * 256])
            for p in range(PAIR):
                for k in range(2):
                    ybuf[g * PAIR + p, 2 * n + k] = y[p * T : (p + 1) * T, k * 128 : (k + 1) * 128]
            if n == 0:
                for p in range(PAIR):
                    far_hop(g * PAIR + p)

    def hops(g, hop):
        for p in range(PAIR):
            next_hop(g * PAIR + p, hop)

    begin(0)
    begin(1)
    for r in range(NZ):
        weight_copy(r).wait()
    out(0)
    begin(2)
    out(1)
    hops(0, 1)
    begin(3)
    for d in ORDER:
        send_return(d, 0)
    rt_recv[me] = return_lane(me)
    out(2)
    hops(1, 1)
    hops(0, 2)
    out(3)
    for g, hop in ((2, 1), (1, 2), (3, 1), (0, 3), (2, 2), (1, 3), (3, 2), (2, 3), (3, 3)):
        hops(g, hop)

    def wait_return(d, carry):
        rt_copy(d).wait()
        return carry

    lax.fori_loop(1, NC, wait_return, 0)

    def leave(s):
        return pltpu.make_async_copy(new_state.at[s], new_state_out.at[s], out_s.at[s])

    def store(s, carry):
        source = jnp.int32(0)
        found = jnp.int32(0)
        for d in range(NC):
            hit = (serve_slot[d] == s) & (serve_live[d] == 1)
            source = jnp.where(hit, d, source)
            found = jnp.where(hit, 1, found)
        came = rt_recv[source].astype(F32)
        fresh = found == 1
        new_state[s] = jnp.where(fresh, came[: 2 * DK], state[s])
        convl[s] = jnp.where(fresh, came[2 * DK :], convl[s])
        leave(s).start()
        return carry

    lax.fori_loop(0, SLOTS, store, 0)
    for s in range(SLOTS):
        for i in range(3):
            for b in range(4):
                newcf[i, s : s + 1, b * 128 : (b + 1) * 128] = convl[s, i * 4 + b : i * 4 + b + 1, :]
    new_conv[...] = newcf[...].astype(BF16)

    def last(j, carry):
        ring_copy(j, 0, 3).wait()
        ring_copy(j, 1, 3).wait()
        total = ybuf[j, 4] + rrecv[j, 0, 3].astype(F32) + rrecv[j, 1, 3].astype(F32)
        layer_out[j] = total.astype(BF16)
        return carry

    lax.fori_loop(0, CONVS, last, 0)

    def left(s, carry):
        leave(s).wait()
        return carry

    lax.fori_loop(0, SLOTS, left, 0)


def hand_on(layer_in, state_in, conv_in, layer_out, state_out, conv_out, layer, state, conv, came, gone):
    parts = [(layer_in, layer, layer_out), (conv_in, conv, conv_out)]
    for n in range(8):
        part = pl.ds(2 * n, 2)
        parts.append((state_in.at[part], state.at[part], state_out.at[part]))
    take = [pltpu.make_async_copy(a, b, came.at[n]) for n, (a, b, _) in enumerate(parts)]
    give = [pltpu.make_async_copy(b, c, gone.at[n]) for n, (_, b, c) in enumerate(parts)]
    for copy in take:
        copy.start()
    for here, there in zip(take, give):
        here.wait()
        there.start()
    for copy in give:
        copy.wait()


def local(
    hidden,
    lengths,
    owners,
    slot_ids,
    state_cache,
    conv_cache,
    w_qkvz,
    w_beta_alpha,
    conv_weight,
    decay_log,
    step_bias,
    norm_gain,
    w_out,
):
    vmem = pl.BlockSpec(memory_space=pltpu.VMEM)
    smem = pl.BlockSpec(memory_space=pltpu.SMEM)
    dma = pltpu.SemaphoreType.DMA
    far = pl.BlockSpec(memory_space=pl.ANY)
    hbm = pl.BlockSpec(memory_space=pltpu.HBM)
    results = (
        jax.ShapeDtypeStruct((CONVS, T, 128), BF16),
        jax.ShapeDtypeStruct((SLOTS, 2 * DK, T), F32),
        jax.ShapeDtypeStruct((3, SLOTS, CH), BF16),
    )
    worked = pl.pallas_call(
        kernel,
        out_shape=results,
        in_specs=[far, smem, smem, smem, far, vmem, far, vmem, vmem, smem, smem, vmem, far],
        out_specs=(vmem, far, vmem),
        scratch_shapes=[
            pltpu.VMEM((CONVS, T, 2048), BF16),
            pltpu.VMEM((SLOTS, 2 * DK, 128), F32),
            pltpu.VMEM((2048, 768), BF16),
            pltpu.VMEM((256, 2048), BF16),
            pltpu.VMEM((SLOTS, 2 * DK, 128), F32),
            dma((4,)),
            dma((SLOTS,)),
            pltpu.VMEM((SLOTS, 16, 128), F32),
            pltpu.VMEM((128, 2048), F32),
            pltpu.VMEM((CONVS, T, 768), BF16),
            pltpu.VMEM((CONVS, T, 128), F32),
            pltpu.SMEM((NC,), jnp.int32),
            pltpu.SMEM((NC,), jnp.int32),
            pltpu.VMEM((NC, 16, 128), BF16),
            pltpu.VMEM((NC, 16, 128), BF16),
            pltpu.VMEM((NC, 2 * DK, 128), BF16),
            pltpu.VMEM((NC, 2 * DK, 128), BF16),
            pltpu.VMEM((PREP, 8 + T, CH), F32),
            pltpu.VMEM((PREP, 16, 128), F32),
            pltpu.VMEM((2 * CONVS, 2 * T, DK), BF16),
            pltpu.VMEM((2 * CONVS, 2 * T, DK), BF16),
            pltpu.VMEM((2 * CONVS, T, DK), F32),
            pltpu.VMEM((CONVS, T, 2 * DK), F32),
            pltpu.VMEM((2 * CONVS, 8, 128), F32),
            pltpu.VMEM((CONVS, 2 * DK + 16, 128), BF16),
            pltpu.VMEM((CONVS, T, 2 * DK), BF16),
            pltpu.VMEM((NC, 2 * DK + 16, 128), BF16),
            pltpu.VMEM((NC, 2 * DK + 16, 128), BF16),
            pltpu.VMEM((CONVS, T, 2 * DK), BF16),
            pltpu.VMEM((512, 1024), BF16),
            pltpu.VMEM((CONVS, NZ, T, 128), F32),
            pltpu.VMEM((CONVS, 2, 4, T, 128), BF16),
            pltpu.VMEM((CONVS, 2, 4, T, 128), BF16),
            pltpu.VMEM((3, SLOTS, CH), F32),
            dma((NC,)),
            dma((NC,)),
            dma((NC,)),
            dma((NC,)),
            dma((NC,)),
            dma((NC,)),
            dma((CONVS // PAIR,)),
            dma((CONVS // PAIR,)),
            dma((NZ,)),
            dma((NZ,)),
            dma((CONVS, 2, 4)),
            dma((CONVS, 2, 4)),
        ],
        compiler_params=pltpu.CompilerParams(
            collective_id=0, has_side_effects=True, vmem_limit_bytes=56 * 1024 * 1024
        ),
    )(
        hidden,
        lengths,
        owners,
        slot_ids,
        state_cache.reshape(SLOTS, 2 * DK, 128),
        conv_cache.transpose(1, 2, 0, 3).reshape(3, SLOTS, CH),
        w_qkvz.reshape(2048, 768),
        w_beta_alpha.transpose(1, 2, 0).reshape(4, 2048),
        conv_weight.reshape(4, CH),
        decay_log,
        step_bias,
        norm_gain.reshape(1, 128),
        w_out,
    )
    layer_out, new_state, new_conv = pl.pallas_call(
        hand_on,
        out_shape=results,
        in_specs=[hbm, hbm, hbm],
        out_specs=(hbm, hbm, hbm),
        scratch_shapes=[pltpu.VMEM(r.shape, r.dtype) for r in results] + [dma((10,)), dma((10,))],
    )(*worked)
    return (
        layer_out,
        new_state.reshape(state_cache.shape),
        new_conv.reshape(3, 1, SLOTS, CH).transpose(2, 0, 1, 3),
    )


def solution(mesh):
    return jax.shard_map(
        local,
        mesh=mesh,
        in_specs=(
            P("cache", None, None),
            P(),
            P(),
            P(),
            P("cache", "tensor", None, None),
            P("cache", None, "tensor", None),
            P(None, "tensor", None),
            P(None, "tensor", None),
            P(None, "tensor", None),
            P("tensor"),
            P("tensor"),
            P(),
            P("tensor", None),
        ),
        out_specs=(
            P("cache", None, "tensor"),
            P("cache", "tensor", None, None),
            P("cache", None, "tensor", None),
        ),
        check_vma=False,
    )
```

```python
import functools
import math

import jax
import jax.numpy as jnp
from jax import lax
from jax.experimental import pallas as pl
from jax.experimental.pallas import tpu as pltpu
from jax.sharding import PartitionSpec as P

F32, BF16 = jnp.float32, jnp.bfloat16
MESH = pl.DeviceIdType.MESH

NC = 16
NZ = 8
CONVS = 8
T = 128
DK = 128
CH = 512
SLOTS = 16
EARLY = 2
PAIR = 2
STEP = 2
PREP = 4
ORDER = sorted(range(1, NC), key=lambda n: -(min(n // 4, 4 - n // 4) + min(n % 4, 4 - n % 4)))


def mm(a, b, ca=1, cb=0):
    return lax.dot_general(
        a.astype(BF16), b.astype(BF16), (((ca,), (cb,)), ((), ())), preferred_element_type=F32
    )


def silu(v):
    return v * (0.5 * jnp.tanh(0.5 * v) + 0.5)


def kernel(
    hidden_in,
    lengths,
    owners,
    slots,
    state_in,
    conv_cache,
    w_qkvz_in,
    w_ba,
    conv_weight,
    decay_log,
    step_bias,
    norm_gain,
    w_out_in,
    layer_out,
    new_state_out,
    new_conv,
    hidden,
    state,
    w_qkvz,
    w_out,
    new_state,
    layer,
    in_s,
    out_s,
    convl,
    wbp,
    proj,
    gate,
    serve_slot,
    serve_live,
    cv_send,
    cv_recv,
    st_send,
    st_recv,
    ext,
    tail_tmp,
    wq,
    pk,
    u0,
    zg,
    eg_end,
    fin,
    nrm,
    rt_send,
    rt_recv,
    nrm_other,
    w_pair,
    ybuf,
    rsend0,
    rrecv0,
    rsend,
    rrecv,
    newcf,
    cv_ss,
    cv_rs,
    st_ss,
    st_rs,
    rt_ss,
    rt_rs,
    nx_ss,
    nx_rs,
    co_ss,
    co_rs,
    ri_ss,
    ri_rs,
):
    me = lax.axis_index("cache")
    tt = lax.axis_index("tensor")
    z = tt // 2
    c = lax.rem(tt, 2)
    other = (me, z * 2 + 1 - c)
    up = (me, lax.rem(z + 1, NZ) * 2 + c)
    down = (me, lax.rem(z + NZ - 1, NZ) * 2 + c)

    def ahead(n):
        return lax.rem(me // 4 + n // 4, 4) * 4 + lax.rem(lax.rem(me, 4) + lax.rem(n, 4), 4)

    loads = [
        pltpu.make_async_copy(src, dst, in_s.at[n])
        for n, (src, dst) in enumerate(
            [(state_in, state), (w_out_in, w_out), (w_qkvz_in, w_qkvz), (hidden_in, hidden)]
        )
    ]
    for load in loads:
        load.start()

    barrier = pltpu.get_barrier_semaphore()

    def greet(d, carry):
        pl.semaphore_signal(barrier, inc=1, device_id=(ahead(d), tt), device_id_type=MESH)
        return carry

    lax.fori_loop(1, NC, greet, 0)
    for peer in (other, up, down):
        pl.semaphore_signal(barrier, inc=1, device_id=peer, device_id_type=MESH)
    newcf[...] = conv_cache[...].astype(F32)
    convl[...] = jnp.zeros_like(convl)
    for s in range(SLOTS):
        for i in range(3):
            for b in range(4):
                convl[s, i * 4 + b : i * 4 + b + 1, :] = newcf[i, s : s + 1, b * 128 : (b + 1) * 128]

    def cv_copy(d):
        peer = ahead(d)
        return pltpu.make_async_remote_copy(
            src_ref=cv_send.at[peer],
            dst_ref=cv_recv.at[me],
            send_sem=cv_ss,
            recv_sem=cv_rs,
            device_id=(peer, tt),
            device_id_type=MESH,
        )

    def st_copy(d):
        peer = ahead(d)
        return pltpu.make_async_remote_copy(
            src_ref=st_send.at[peer],
            dst_ref=st_recv.at[me],
            send_sem=st_ss,
            recv_sem=st_rs,
            device_id=(peer, tt),
            device_id_type=MESH,
        )

    def settle(sent, came, send_sem, recv_sem):
        lanes = pl.ds(0, NC - 1)
        pltpu.make_async_remote_copy(
            src_ref=sent.at[lanes],
            dst_ref=came.at[lanes],
            send_sem=send_sem,
            recv_sem=recv_sem,
            device_id=(ahead(1), tt),
            device_id_type=MESH,
        ).wait()

    def conv_lane(peer):
        slot = jnp.int32(0)
        live = jnp.int32(0)
        for j in range(CONVS):
            hit = owners[peer * CONVS + j] == me
            slot = jnp.where(hit, slots[peer * CONVS + j], slot)
            live = jnp.where(hit, 1, live)
        serve_slot[peer] = slot
        serve_live[peer] = live
        return convl[slot].astype(BF16)

    tail_tmp[...] = jnp.zeros_like(tail_tmp)

    def pack_conv(peer, carry):
        cv_send[peer] = conv_lane(peer)
        return carry

    lax.fori_loop(0, NC, pack_conv, 0)
    cv_recv[me] = cv_send[me]
    pl.semaphore_wait(barrier, NC - 1 + 3)

    def send_conv(d, carry):
        cv_copy(d).start()
        return carry

    lax.fori_loop(1, NC, send_conv, 0)

    loads[0].wait()

    for n, d in enumerate(ORDER):
        peer = ahead(d)
        st_send[peer] = state[serve_slot[peer]].astype(BF16)
        if n < EARLY:
            st_copy(d).start()
    st_recv[me] = state[serve_slot[me]].astype(BF16)

    def columns(r, core):
        return pl.ds(pl.multiple_of((lax.rem(z + 4 + r, NZ) * 2 + core) * 128, 128), 128)

    def weight_copy(r):
        return pltpu.make_async_remote_copy(
            src_ref=w_out.at[:, columns(r, 1 - c)],
            dst_ref=w_pair.at[pl.ds(256, 256), pl.ds(r * 128, 128)],
            send_sem=co_ss,
            recv_sem=co_rs,
            device_id=other,
            device_id_type=MESH,
        )

    loads[1].wait()
    for r in range(NZ):
        weight_copy(r).start()
    for r in range(NZ):
        w_pair[0:256, r * 128 : (r + 1) * 128] = w_out[:, columns(r, c)]

    settle(cv_send, cv_recv, cv_ss, cv_rs)

    for d in ORDER[EARLY:]:
        st_copy(d).start()

    wbp[...] = jnp.zeros_like(wbp)
    wbp[0:4, :] = w_ba[...].astype(F32)
    loads[2].wait()
    loads[3].wait()

    def project(g, carry):
        x = hidden[pl.ds(g * STEP, STEP)].reshape(STEP * T, hidden.shape[-1])
        projected = mm(x, w_qkvz[...]).astype(BF16)
        gates = mm(x, wbp[...], 1, 1).astype(BF16).astype(F32)
        for p in range(STEP):
            proj[g * STEP + p] = projected[p * T : (p + 1) * T]
            gate[g * STEP + p] = gates[p * T : (p + 1) * T]
        return carry

    lax.fori_loop(0, CONVS // STEP, project, 0)

    rows = lax.broadcasted_iota(jnp.int32, (T, T), 0)
    cols = lax.broadcasted_iota(jnp.int32, (T, T), 1)
    lane = lax.broadcasted_iota(jnp.int32, (1, T), 1)
    pos = lax.broadcasted_iota(jnp.int32, (T, 1), 0)

    def prepare(g, carry):
        rate = jnp.exp(
            jnp.where(lane == 2, decay_log[0], jnp.where(lane == 3, decay_log[1], 0.0))
        )
        bias = jnp.where(lane == 2, step_bias[0], jnp.where(lane == 3, step_bias[1], 0.0))
        inclusive = rows >= cols
        strictly = rows > cols
        tri = jnp.where(inclusive, 1.0, 0.0)
        chains = []
        for p in range(PREP):
            j = g * PREP + p
            length = lengths[me * CONVS + j]
            owner = owners[me * CONVS + j]
            live = pos < length
            mixed = proj[j, :, :CH].astype(F32)
            z_part = proj[j, :, CH:].astype(F32)
            held = cv_recv[owner].astype(F32)
            for i in range(3):
                for b in range(4):
                    ext[p, 5 + i : 6 + i, b * 128 : (b + 1) * 128] = held[i * 4 + b : i * 4 + b + 1, :]
            ext[p, 8 : 8 + T, :] = mixed
            convolved = conv_weight[3:4, :].astype(F32) * mixed
            for i in range(3):
                convolved = convolved + conv_weight[i : i + 1, :].astype(F32) * ext[p, 5 + i : 5 + i + T, :]
            for i in range(3):
                row = ext[p, pl.ds(5 + length + i, 1), :]
                for b in range(4):
                    tail_tmp[p, i * 4 + b : i * 4 + b + 1, :] = row[:, b * 128 : (b + 1) * 128]
            fin[j, 2 * DK : 2 * DK + 16, :] = tail_tmp[p].astype(BF16)
            act = silu(convolved)
            q = act[:, :DK]
            k = act[:, DK : 2 * DK]
            q = q * lax.rsqrt(jnp.sum(q * q, axis=-1, keepdims=True) + 1e-06) * (1.0 / math.sqrt(DK))
            k = k * lax.rsqrt(jnp.sum(k * k, axis=-1, keepdims=True) + 1e-06)
            zg[j] = jnp.where(
                live,
                silu(z_part) * jnp.concatenate([norm_gain[...], norm_gain[...]], axis=1),
                0.0,
            )
            raw = gate[j]
            beta = jnp.where(live, 0.5 * jnp.tanh(0.5 * raw) + 0.5, 0.0)
            shifted = raw + bias
            decay = jnp.where(
                live,
                -rate * (jnp.maximum(shifted, 0.0) + jnp.log1p(jnp.exp(-jnp.abs(shifted)))),
                0.0,
            )
            total = jnp.dot(tri, decay, precision=lax.Precision.HIGHEST, preferred_element_type=F32)
            total_rows = total.T
            qk = mm(jnp.concatenate([k, q], axis=0), k, 1, 1)
            k_t = k.T
            for h in range(2):
                gc = total[:, 2 + h : 3 + h]
                gr = total_rows[2 + h : 3 + h, :]
                g_end = gr[:, T - 1 : T]
                bc = beta[:, h : h + 1]
                gap = jnp.where(inclusive, jnp.exp(jnp.where(inclusive, gc - gr, 0.0)), 0.0)
                lower = jnp.where(strictly, bc * qk[:T] * gap, 0.0)
                grow = jnp.exp(gc)
                wq[2 * j + h, T:, :] = (q * grow).astype(BF16)
                pk[2 * j + h, :T, :] = (qk[T:] * gap).astype(BF16)
                pk[2 * j + h, T:, :] = (k_t * jnp.exp(g_end - gr)).astype(BF16)
                eg_end[2 * j + h] = jnp.broadcast_to(jnp.exp(g_end), (8, T))
                right = jnp.concatenate(
                    [(bc * grow * k), bc * act[:, 2 * DK + h * T : 2 * DK + (h + 1) * T]], axis=1
                ).astype(BF16)
                chains.append((2 * j + h, lower, right))
        inverse = [
            jnp.where(rows == cols, 1.0, 0.0) - jnp.where(rows // 2 == cols // 2, low, 0.0)
            for _, low, _ in chains
        ]
        span = 2
        while span < T:
            block = (rows // (4 * span) == cols // (4 * span)) & (rows // span != cols // span)
            nil = [mm(inv, jnp.where(block, low, 0.0)) for (_, low, _), inv in zip(chains, inverse)]
            square = [mm(n, n) for n in nil]
            first = [inv - mm(n, inv) for n, inv in zip(nil, inverse)]
            inverse = [f + mm(q, f) for q, f in zip(square, first)]
            span *= 4
        for (at, _, right), inv in zip(chains, inverse):
            solved = mm(inv, right)
            wq[at, :T, :] = solved[:, :DK].astype(BF16)
            u0[at] = solved[:, DK:]
        return carry

    lax.fori_loop(0, CONVS // PREP, prepare, 0)

    settle(st_send, st_recv, st_ss, st_rs)

    def finish(g, carry):
        for p in range(PAIR):
            j = g * PAIR + p
            owner = owners[me * CONVS + j]
            for h in range(2):
                at = 2 * j + h
                memory = st_recv[owner, h * DK : (h + 1) * DK, :]
                seen = mm(wq[at], memory)
                update = u0[at] - seen[:T]
                given = mm(pk[at], update)
                core = seen[T:] + given[:T]
                after = eg_end[at][0:1, :] * memory.astype(F32) + given[T:]
                fin[j, h * DK : (h + 1) * DK, :] = after.astype(BF16)
                scale = lax.rsqrt(jnp.mean(core * core, axis=-1, keepdims=True) + 1e-06)
                nrm[j, :, h * DK : (h + 1) * DK] = (
                    core * scale * zg[j, :, h * DK : (h + 1) * DK]
                ).astype(BF16)
        return carry

    def rt_copy(d):
        peer = ahead(d)
        return pltpu.make_async_remote_copy(
            src_ref=rt_send.at[peer],
            dst_ref=rt_recv.at[me],
            send_sem=rt_ss,
            recv_sem=rt_rs,
            device_id=(peer, tt),
            device_id_type=MESH,
        )

    def return_lane(peer):
        pick = jnp.int32(0)
        for j in range(CONVS):
            pick = jnp.where(owners[me * CONVS + j] == peer, j, pick)
        return fin[pick]

    def send_return(d, carry):
        peer = ahead(d)
        rt_send[peer] = return_lane(peer)
        rt_copy(d).start()
        return carry

    def norm_copy(g):
        pair = pl.ds(g * PAIR, PAIR)
        return pltpu.make_async_remote_copy(
            src_ref=nrm.at[pair],
            dst_ref=nrm_other.at[pair],
            send_sem=nx_ss,
            recv_sem=nx_rs.at[g],
            device_id=other,
            device_id_type=MESH,
        )

    def ring_copy(src, dst, way, g, hop):
        return pltpu.make_async_remote_copy(
            src_ref=src,
            dst_ref=dst,
            send_sem=ri_ss.at[min(hop, 1)],
            recv_sem=ri_rs.at[g, hop],
            device_id=up if way == 0 else down,
            device_id_type=MESH,
        )

    half = T // 2

    def far_hop(j, g):
        far = ybuf[j, 0].astype(BF16)
        for way in (0, 1):
            rsend0[j, way] = far[way * half : (way + 1) * half]
            ring_copy(rsend0.at[j, way], rrecv0.at[j, way], way, g, 0).start()

    def came(g, hop):
        pair = pl.ds(g * PAIR, PAIR)
        ref = rrecv0.at[pair] if hop == 0 else rrecv.at[hop - 1, pair]
        ring_copy(ref, ref, 0, g, hop).wait_recv()

    def next_hop(j, g, hop):
        for way in (0, 1):
            mine = ybuf[j, NZ - hop if way == 0 else hop]
            if hop == 1:
                keep = slice(way * half, (way + 1) * half)
                alone = slice((1 - way) * half, (2 - way) * half)
                rsend[0, j, way, keep, :] = (mine[keep] + rrecv0[j, way].astype(F32)).astype(BF16)
                rsend[0, j, way, alone, :] = mine[alone].astype(BF16)
            else:
                rsend[hop - 1, j, way] = (mine + rrecv[hop - 2, j, way].astype(F32)).astype(BF16)
            ring_copy(rsend.at[hop - 1, j, way], rrecv.at[hop - 1, j, way], way, g, hop).start()

    def begin(g):
        finish(g, 0)
        norm_copy(g).start()

    def out(g):
        norm_copy(g).wait_recv()
        pair = pl.ds(g * PAIR, PAIR)
        x = jnp.concatenate([nrm[pair].reshape(PAIR * T, 256), nrm_other[pair].reshape(PAIR * T, 256)], axis=1)
        for n in range(NZ // 2):
            y = mm(x, w_pair[:, n * 256 : (n + 1) * 256])
            for p in range(PAIR):
                for k in range(2):
                    ybuf[g * PAIR + p, 2 * n + k] = y[p * T : (p + 1) * T, k * 128 : (k + 1) * 128]
            if n == 0:
                for p in range(PAIR):
                    far_hop(g * PAIR + p, g)

    def hops(g, hop):
        came(g, hop - 1)
        for p in range(PAIR):
            next_hop(g * PAIR + p, g, hop)

    begin(0)
    begin(1)
    rows_other = w_pair.at[pl.ds(256, 256)]
    pltpu.make_async_remote_copy(
        src_ref=rows_other,
        dst_ref=rows_other,
        send_sem=co_ss,
        recv_sem=co_rs,
        device_id=other,
        device_id_type=MESH,
    ).wait()
    out(0)
    begin(2)
    out(1)
    hops(0, 1)
    begin(3)
    for d in ORDER:
        send_return(d, 0)
    rt_recv[me] = return_lane(me)
    out(2)
    hops(1, 1)
    hops(0, 2)
    out(3)
    for g, hop in ((2, 1), (1, 2), (3, 1), (0, 3), (2, 2), (1, 3), (3, 2), (2, 3), (3, 3)):
        hops(g, hop)

    settle(rt_send, rt_recv, rt_ss, rt_rs)

    def leave(s):
        return pltpu.make_async_copy(new_state.at[s], new_state_out.at[s], out_s.at[0])

    def store(s, carry):
        source = jnp.int32(0)
        found = jnp.int32(0)
        for d in range(NC):
            hit = (serve_slot[d] == s) & (serve_live[d] == 1)
            source = jnp.where(hit, d, source)
            found = jnp.where(hit, 1, found)
        came = rt_recv[source].astype(F32)
        fresh = found == 1
        new_state[s] = jnp.where(fresh, came[: 2 * DK], state[s])
        convl[s] = jnp.where(fresh, came[2 * DK :], convl[s])
        leave(s).start()
        return carry

    lax.fori_loop(0, SLOTS, store, 0)
    for s in range(SLOTS):
        for i in range(3):
            for b in range(4):
                newcf[i, s : s + 1, b * 128 : (b + 1) * 128] = convl[s, i * 4 + b : i * 4 + b + 1, :]
    new_conv[...] = newcf[...].astype(BF16)

    for g in range(CONVS // PAIR):
        came(g, 3)
        for p in range(PAIR):
            j = g * PAIR + p
            total = ybuf[j, 4] + rrecv[2, j, 0].astype(F32) + rrecv[2, j, 1].astype(F32)
            layer[j] = total.astype(BF16)
        pair = pl.ds(g * PAIR, PAIR)
        pltpu.make_async_copy(layer.at[pair], layer_out.at[pair], out_s.at[1]).start()

    ring_copy(rsend0, rrecv0, 0, 0, 0).wait_send()
    ring_copy(rsend, rrecv, 0, 0, 1).wait_send()
    pltpu.make_async_remote_copy(
        src_ref=nrm,
        dst_ref=nrm_other,
        send_sem=nx_ss,
        recv_sem=nx_rs.at[0],
        device_id=other,
        device_id_type=MESH,
    ).wait_send()
    pltpu.make_async_copy(new_state, new_state_out, out_s.at[0]).wait()
    pltpu.make_async_copy(layer, layer_out, out_s.at[1]).wait()


def hand_on(layer_in, state_in, conv_in, layer_out, state_out, conv_out, layer, state, conv, came, gone):
    parts = [(layer_in, layer, layer_out), (conv_in, conv, conv_out)]
    for n in range(8):
        part = pl.ds(2 * n, 2)
        parts.append((state_in.at[part], state.at[part], state_out.at[part]))
    take = [pltpu.make_async_copy(a, b, came.at[n]) for n, (a, b, _) in enumerate(parts)]
    give = [pltpu.make_async_copy(b, c, gone.at[n]) for n, (_, b, c) in enumerate(parts)]
    for copy in take:
        copy.start()
    for here, there in zip(take, give):
        here.wait()
        there.start()
    for copy in give:
        copy.wait()


def local(
    hidden,
    lengths,
    owners,
    slot_ids,
    state_cache,
    conv_cache,
    w_qkvz,
    w_beta_alpha,
    conv_weight,
    decay_log,
    step_bias,
    norm_gain,
    w_out,
):
    vmem = pl.BlockSpec(memory_space=pltpu.VMEM)
    smem = pl.BlockSpec(memory_space=pltpu.SMEM)
    dma = pltpu.SemaphoreType.DMA
    far = pl.BlockSpec(memory_space=pl.ANY)
    hbm = pl.BlockSpec(memory_space=pltpu.HBM)
    results = (
        jax.ShapeDtypeStruct((CONVS, T, 128), BF16),
        jax.ShapeDtypeStruct((SLOTS, 2 * DK, T), F32),
        jax.ShapeDtypeStruct((3, SLOTS, CH), BF16),
    )
    worked = pl.pallas_call(
        kernel,
        out_shape=results,
        in_specs=[far, smem, smem, smem, far, vmem, far, vmem, vmem, smem, smem, vmem, far],
        out_specs=(far, far, vmem),
        scratch_shapes=[
            pltpu.VMEM((CONVS, T, 2048), BF16),
            pltpu.VMEM((SLOTS, 2 * DK, 128), F32),
            pltpu.VMEM((2048, 768), BF16),
            pltpu.VMEM((256, 2048), BF16),
            pltpu.VMEM((SLOTS, 2 * DK, 128), F32),
            pltpu.VMEM((CONVS, T, 128), BF16),
            dma((4,)),
            dma((2,)),
            pltpu.VMEM((SLOTS, 16, 128), F32),
            pltpu.VMEM((128, 2048), F32),
            pltpu.VMEM((CONVS, T, 768), BF16),
            pltpu.VMEM((CONVS, T, 128), F32),
            pltpu.SMEM((NC,), jnp.int32),
            pltpu.SMEM((NC,), jnp.int32),
            pltpu.VMEM((NC, 16, 128), BF16),
            pltpu.VMEM((NC, 16, 128), BF16),
            pltpu.VMEM((NC, 2 * DK, 128), BF16),
            pltpu.VMEM((NC, 2 * DK, 128), BF16),
            pltpu.VMEM((PREP, 8 + T, CH), F32),
            pltpu.VMEM((PREP, 16, 128), F32),
            pltpu.VMEM((2 * CONVS, 2 * T, DK), BF16),
            pltpu.VMEM((2 * CONVS, 2 * T, DK), BF16),
            pltpu.VMEM((2 * CONVS, T, DK), F32),
            pltpu.VMEM((CONVS, T, 2 * DK), F32),
            pltpu.VMEM((2 * CONVS, 8, 128), F32),
            pltpu.VMEM((CONVS, 2 * DK + 16, 128), BF16),
            pltpu.VMEM((CONVS, T, 2 * DK), BF16),
            pltpu.VMEM((NC, 2 * DK + 16, 128), BF16),
            pltpu.VMEM((NC, 2 * DK + 16, 128), BF16),
            pltpu.VMEM((CONVS, T, 2 * DK), BF16),
            pltpu.VMEM((512, 1024), BF16),
            pltpu.VMEM((CONVS, NZ, T, 128), F32),
            pltpu.VMEM((CONVS, 2, T // 2, 128), BF16),
            pltpu.VMEM((CONVS, 2, T // 2, 128), BF16),
            pltpu.VMEM((3, CONVS, 2, T, 128), BF16),
            pltpu.VMEM((3, CONVS, 2, T, 128), BF16),
            pltpu.VMEM((3, SLOTS, CH), F32),
            dma(()),
            dma(()),
            dma(()),
            dma(()),
            dma(()),
            dma(()),
            dma(()),
            dma((CONVS // PAIR,)),
            dma(()),
            dma(()),
            dma((2,)),
            dma((CONVS // PAIR, 4)),
        ],
        compiler_params=pltpu.CompilerParams(
            collective_id=0, has_side_effects=True, vmem_limit_bytes=56 * 1024 * 1024
        ),
    )(
        hidden,
        lengths,
        owners,
        slot_ids,
        state_cache.reshape(SLOTS, 2 * DK, 128),
        conv_cache.transpose(1, 2, 0, 3).reshape(3, SLOTS, CH),
        w_qkvz.reshape(2048, 768),
        w_beta_alpha.transpose(1, 2, 0).reshape(4, 2048),
        conv_weight.reshape(4, CH),
        decay_log,
        step_bias,
        norm_gain.reshape(1, 128),
        w_out,
    )
    layer_out, new_state, new_conv = pl.pallas_call(
        hand_on,
        out_shape=results,
        in_specs=[hbm, hbm, hbm],
        out_specs=(hbm, hbm, hbm),
        scratch_shapes=[pltpu.VMEM(r.shape, r.dtype) for r in results] + [dma((10,)), dma((10,))],
    )(*worked)
    return (
        layer_out,
        new_state.reshape(state_cache.shape),
        new_conv.reshape(3, 1, SLOTS, CH).transpose(2, 0, 1, 3),
    )


def solution(mesh):
    return jax.shard_map(
        local,
        mesh=mesh,
        in_specs=(
            P("cache", None, None),
            P(),
            P(),
            P(),
            P("cache", "tensor", None, None),
            P("cache", None, "tensor", None),
            P(None, "tensor", None),
            P(None, "tensor", None),
            P(None, "tensor", None),
            P("tensor"),
            P("tensor"),
            P(),
            P("tensor", None),
        ),
        out_specs=(
            P("cache", None, "tensor"),
            P("cache", "tensor", None, None),
            P("cache", None, "tensor", None),
        ),
        check_vma=False,
    )
```

```python
import functools
import math

import jax
import jax.numpy as jnp
from jax import lax
from jax.experimental import pallas as pl
from jax.experimental.pallas import tpu as pltpu
from jax.sharding import PartitionSpec as P

F32, BF16 = jnp.float32, jnp.bfloat16
MESH = pl.DeviceIdType.MESH

NC = 16
NZ = 8
CONVS = 8
T = 128
DK = 128
CH = 512
SLOTS = 16
EARLY = 2
PAIR = 2
STEP = 4
PREP = 8
ORDER = sorted(range(1, NC), key=lambda n: -(min(n // 4, 4 - n // 4) + min(n % 4, 4 - n % 4)))


def mm(a, b, ca=1, cb=0):
    return lax.dot_general(
        a.astype(BF16), b.astype(BF16), (((ca,), (cb,)), ((), ())), preferred_element_type=F32
    )


def silu(v):
    return v * (0.5 * jnp.tanh(0.5 * v) + 0.5)


def kernel(
    hidden_in,
    lengths,
    owners,
    slots,
    state_in,
    conv_cache,
    w_qkvz_in,
    w_ba,
    conv_weight,
    decay_log,
    step_bias,
    norm_gain,
    w_out_in,
    layer_out,
    new_state_out,
    new_conv,
    hidden,
    state,
    w_qkvz,
    w_out,
    new_state,
    layer,
    in_s,
    out_s,
    convl,
    wbp,
    proj,
    gate,
    serve_slot,
    serve_live,
    cv_send,
    cv_recv,
    st_send,
    st_recv,
    ext,
    tail_tmp,
    wq,
    pk,
    u0,
    zg,
    eg_end,
    fin,
    nrm,
    rt_send,
    rt_recv,
    nrm_other,
    w_pair,
    ybuf,
    rsend0,
    rrecv0,
    rsend,
    rrecv,
    newcf,
    cv_ss,
    cv_rs,
    st_ss,
    st_rs,
    rt_ss,
    rt_rs,
    nx_ss,
    nx_rs,
    co_ss,
    co_rs,
    ri_ss,
    ri_rs,
):
    me = lax.axis_index("cache")
    tt = lax.axis_index("tensor")
    z = tt // 2
    c = lax.rem(tt, 2)
    other = (me, z * 2 + 1 - c)
    up = (me, lax.rem(z + 1, NZ) * 2 + c)
    down = (me, lax.rem(z + NZ - 1, NZ) * 2 + c)

    def ahead(n):
        return lax.rem(me // 4 + n // 4, 4) * 4 + lax.rem(lax.rem(me, 4) + lax.rem(n, 4), 4)

    loads = [
        pltpu.make_async_copy(src, dst, in_s.at[n])
        for n, (src, dst) in enumerate(
            [(state_in, state), (w_out_in, w_out), (w_qkvz_in, w_qkvz), (hidden_in, hidden)]
        )
    ]
    for load in loads:
        load.start()

    barrier = pltpu.get_barrier_semaphore()

    def greet(d, carry):
        pl.semaphore_signal(barrier, inc=1, device_id=(ahead(d), tt), device_id_type=MESH)
        return carry

    for d in ORDER:
        greet(d, 0)
    for peer in (other, up, down):
        pl.semaphore_signal(barrier, inc=1, device_id=peer, device_id_type=MESH)
    newcf[...] = conv_cache[...].astype(F32)
    convl[...] = jnp.zeros_like(convl)
    for s in range(SLOTS):
        for i in range(3):
            for b in range(4):
                convl[s, i * 4 + b : i * 4 + b + 1, :] = newcf[i, s : s + 1, b * 128 : (b + 1) * 128]

    def cv_copy(d):
        peer = ahead(d)
        return pltpu.make_async_remote_copy(
            src_ref=cv_send.at[peer],
            dst_ref=cv_recv.at[me],
            send_sem=cv_ss,
            recv_sem=cv_rs,
            device_id=(peer, tt),
            device_id_type=MESH,
        )

    def st_copy(d):
        peer = ahead(d)
        return pltpu.make_async_remote_copy(
            src_ref=st_send.at[peer],
            dst_ref=st_recv.at[me],
            send_sem=st_ss,
            recv_sem=st_rs,
            device_id=(peer, tt),
            device_id_type=MESH,
        )

    def settle(sent, came, send_sem, recv_sem):
        lanes = pl.ds(0, NC - 1)
        pltpu.make_async_remote_copy(
            src_ref=sent.at[lanes],
            dst_ref=came.at[lanes],
            send_sem=send_sem,
            recv_sem=recv_sem,
            device_id=(ahead(1), tt),
            device_id_type=MESH,
        ).wait()

    def conv_lane(peer):
        slot = jnp.int32(0)
        live = jnp.int32(0)
        for j in range(CONVS):
            hit = owners[peer * CONVS + j] == me
            slot = jnp.where(hit, slots[peer * CONVS + j], slot)
            live = jnp.where(hit, 1, live)
        serve_slot[peer] = slot
        serve_live[peer] = live
        return convl[slot].astype(BF16)

    tail_tmp[...] = jnp.zeros_like(tail_tmp)

    def pack_conv(peer, carry):
        cv_send[peer] = conv_lane(peer)
        return carry

    lax.fori_loop(0, NC, pack_conv, 0)
    cv_recv[me] = cv_send[me]
    pl.semaphore_wait(barrier, NC - 1 + 3)

    def send_conv(d, carry):
        cv_copy(d).start()
        return carry

    for d in ORDER:
        send_conv(d, 0)

    loads[0].wait()

    for n, d in enumerate(ORDER):
        peer = ahead(d)
        st_send[peer] = state[serve_slot[peer]].astype(BF16)
        if n < EARLY:
            st_copy(d).start()
    st_recv[me] = state[serve_slot[me]].astype(BF16)

    def columns(r, core):
        return pl.ds(pl.multiple_of((lax.rem(z + 4 + r, NZ) * 2 + core) * 128, 128), 128)

    def weight_copy(r):
        return pltpu.make_async_remote_copy(
            src_ref=w_out.at[:, columns(r, 1 - c)],
            dst_ref=w_pair.at[pl.ds(256, 256), pl.ds(r * 128, 128)],
            send_sem=co_ss,
            recv_sem=co_rs,
            device_id=other,
            device_id_type=MESH,
        )

    loads[1].wait()
    for r in range(NZ):
        weight_copy(r).start()
    for r in range(NZ):
        w_pair[0:256, r * 128 : (r + 1) * 128] = w_out[:, columns(r, c)]

    settle(cv_send, cv_recv, cv_ss, cv_rs)

    for d in ORDER[EARLY:]:
        st_copy(d).start()

    wbp[...] = jnp.zeros_like(wbp)
    wbp[0:4, :] = w_ba[...].astype(F32)
    loads[2].wait()
    loads[3].wait()

    def project(g, carry):
        x = hidden[pl.ds(g * STEP, STEP)].reshape(STEP * T, hidden.shape[-1])
        projected = mm(x, w_qkvz[...]).astype(BF16)
        gates = mm(x, wbp[...], 1, 1).astype(BF16).astype(F32)
        for p in range(STEP):
            proj[g * STEP + p] = projected[p * T : (p + 1) * T]
            gate[g * STEP + p] = gates[p * T : (p + 1) * T]
        return carry

    lax.fori_loop(0, CONVS // STEP, project, 0)

    rows = lax.broadcasted_iota(jnp.int32, (T, T), 0)
    cols = lax.broadcasted_iota(jnp.int32, (T, T), 1)
    lane = lax.broadcasted_iota(jnp.int32, (1, T), 1)
    pos = lax.broadcasted_iota(jnp.int32, (T, 1), 0)

    def prepare(g, carry):
        rate = jnp.exp(
            jnp.where(lane == 2, decay_log[0], jnp.where(lane == 3, decay_log[1], 0.0))
        )
        bias = jnp.where(lane == 2, step_bias[0], jnp.where(lane == 3, step_bias[1], 0.0))
        inclusive = rows >= cols
        strictly = rows > cols
        tri = jnp.where(inclusive, 1.0, 0.0)
        chains = []
        for p in range(PREP):
            j = g * PREP + p
            length = lengths[me * CONVS + j]
            owner = owners[me * CONVS + j]
            live = pos < length
            mixed = proj[j, :, :CH].astype(F32)
            z_part = proj[j, :, CH:].astype(F32)
            held = cv_recv[owner].astype(F32)
            for i in range(3):
                for b in range(4):
                    ext[p, 5 + i : 6 + i, b * 128 : (b + 1) * 128] = held[i * 4 + b : i * 4 + b + 1, :]
            ext[p, 8 : 8 + T, :] = mixed
            convolved = conv_weight[3:4, :].astype(F32) * mixed
            for i in range(3):
                convolved = convolved + conv_weight[i : i + 1, :].astype(F32) * ext[p, 5 + i : 5 + i + T, :]
            for i in range(3):
                row = ext[p, pl.ds(5 + length + i, 1), :]
                for b in range(4):
                    tail_tmp[p, i * 4 + b : i * 4 + b + 1, :] = row[:, b * 128 : (b + 1) * 128]
            fin[j, 2 * DK : 2 * DK + 16, :] = tail_tmp[p].astype(BF16)
            act = silu(convolved)
            q = act[:, :DK]
            k = act[:, DK : 2 * DK]
            q = q * lax.rsqrt(jnp.sum(q * q, axis=-1, keepdims=True) + 1e-06) * (1.0 / math.sqrt(DK))
            k = k * lax.rsqrt(jnp.sum(k * k, axis=-1, keepdims=True) + 1e-06)
            zg[j] = jnp.where(
                live,
                silu(z_part) * jnp.concatenate([norm_gain[...], norm_gain[...]], axis=1),
                0.0,
            )
            raw = gate[j]
            beta = jnp.where(live, 0.5 * jnp.tanh(0.5 * raw) + 0.5, 0.0)
            shifted = raw + bias
            decay = jnp.where(
                live,
                -rate * (jnp.maximum(shifted, 0.0) + jnp.log1p(jnp.exp(-jnp.abs(shifted)))),
                0.0,
            )
            total = jnp.dot(tri, decay, precision=lax.Precision.HIGHEST, preferred_element_type=F32)
            total_rows = total.T
            qk = mm(jnp.concatenate([k, q], axis=0), k, 1, 1)
            k_t = k.T
            for h in range(2):
                gc = total[:, 2 + h : 3 + h]
                gr = total_rows[2 + h : 3 + h, :]
                g_end = gr[:, T - 1 : T]
                bc = beta[:, h : h + 1]
                gap = jnp.where(inclusive, jnp.exp(jnp.where(inclusive, gc - gr, 0.0)), 0.0)
                lower = jnp.where(strictly, bc * qk[:T] * gap, 0.0)
                grow = jnp.exp(gc)
                wq[2 * j + h, T:, :] = (q * grow).astype(BF16)
                pk[2 * j + h, :T, :] = (qk[T:] * gap).astype(BF16)
                pk[2 * j + h, T:, :] = (k_t * jnp.exp(g_end - gr)).astype(BF16)
                eg_end[2 * j + h] = jnp.broadcast_to(jnp.exp(g_end), (8, T))
                right = jnp.concatenate(
                    [(bc * grow * k), bc * act[:, 2 * DK + h * T : 2 * DK + (h + 1) * T]], axis=1
                ).astype(BF16)
                chains.append((2 * j + h, lower, right))
        inverse = [
            jnp.where(rows == cols, 1.0, 0.0) - jnp.where(rows // 2 == cols // 2, low, 0.0)
            for _, low, _ in chains
        ]
        span = 2
        while span < T:
            block = (rows // (4 * span) == cols // (4 * span)) & (rows // span != cols // span)
            nil = [mm(inv, jnp.where(block, low, 0.0)) for (_, low, _), inv in zip(chains, inverse)]
            square = [mm(n, n) for n in nil]
            first = [inv - mm(n, inv) for n, inv in zip(nil, inverse)]
            inverse = [f + mm(q, f) for q, f in zip(square, first)]
            span *= 4
        for (at, _, right), inv in zip(chains, inverse):
            solved = mm(inv, right)
            wq[at, :T, :] = solved[:, :DK].astype(BF16)
            u0[at] = solved[:, DK:]
        return carry

    lax.fori_loop(0, CONVS // PREP, prepare, 0)

    settle(st_send, st_recv, st_ss, st_rs)

    def finish(g, carry):
        for p in range(PAIR):
            j = g * PAIR + p
            owner = owners[me * CONVS + j]
            for h in range(2):
                at = 2 * j + h
                memory = st_recv[owner, h * DK : (h + 1) * DK, :]
                seen = mm(wq[at], memory)
                update = u0[at] - seen[:T]
                given = mm(pk[at], update)
                core = seen[T:] + given[:T]
                after = eg_end[at][0:1, :] * memory.astype(F32) + given[T:]
                fin[j, h * DK : (h + 1) * DK, :] = after.astype(BF16)
                scale = lax.rsqrt(jnp.mean(core * core, axis=-1, keepdims=True) + 1e-06)
                nrm[j, :, h * DK : (h + 1) * DK] = (
                    core * scale * zg[j, :, h * DK : (h + 1) * DK]
                ).astype(BF16)
        return carry

    def rt_copy(d):
        peer = ahead(d)
        return pltpu.make_async_remote_copy(
            src_ref=rt_send.at[peer],
            dst_ref=rt_recv.at[me],
            send_sem=rt_ss,
            recv_sem=rt_rs,
            device_id=(peer, tt),
            device_id_type=MESH,
        )

    def return_lane(peer):
        pick = jnp.int32(0)
        for j in range(CONVS):
            pick = jnp.where(owners[me * CONVS + j] == peer, j, pick)
        return fin[pick]

    def send_return(d, carry):
        peer = ahead(d)
        rt_send[peer] = return_lane(peer)
        rt_copy(d).start()
        return carry

    def norm_copy(g):
        pair = pl.ds(g * PAIR, PAIR)
        return pltpu.make_async_remote_copy(
            src_ref=nrm.at[pair],
            dst_ref=nrm_other.at[pair],
            send_sem=nx_ss,
            recv_sem=nx_rs.at[g],
            device_id=other,
            device_id_type=MESH,
        )

    def ring_copy(src, dst, way, g, hop):
        return pltpu.make_async_remote_copy(
            src_ref=src,
            dst_ref=dst,
            send_sem=ri_ss.at[min(hop, 1)],
            recv_sem=ri_rs.at[g, hop],
            device_id=up if way == 0 else down,
            device_id_type=MESH,
        )

    half = T // 2

    def far_hop(j, g):
        far = ybuf[j, 0].astype(BF16)
        for way in (0, 1):
            rsend0[j, way] = far[way * half : (way + 1) * half]
            ring_copy(rsend0.at[j, way], rrecv0.at[j, way], way, g, 0).start()

    def came(g, hop):
        pair = pl.ds(g * PAIR, PAIR)
        ref = rrecv0.at[pair] if hop == 0 else rrecv.at[hop - 1, pair]
        ring_copy(ref, ref, 0, g, hop).wait_recv()

    def next_hop(j, g, hop):
        for way in (0, 1):
            mine = ybuf[j, NZ - hop if way == 0 else hop]
            if hop == 1:
                keep = slice(way * half, (way + 1) * half)
                alone = slice((1 - way) * half, (2 - way) * half)
                rsend[0, j, way, keep, :] = (mine[keep] + rrecv0[j, way].astype(F32)).astype(BF16)
                rsend[0, j, way, alone, :] = mine[alone].astype(BF16)
            else:
                rsend[hop - 1, j, way] = (mine + rrecv[hop - 2, j, way].astype(F32)).astype(BF16)
            ring_copy(rsend.at[hop - 1, j, way], rrecv.at[hop - 1, j, way], way, g, hop).start()

    def begin(g):
        finish(g, 0)
        norm_copy(g).start()

    def out(g):
        norm_copy(g).wait_recv()
        pair = pl.ds(g * PAIR, PAIR)
        x = jnp.concatenate([nrm[pair].reshape(PAIR * T, 256), nrm_other[pair].reshape(PAIR * T, 256)], axis=1)
        for n in range(NZ // 2):
            y = mm(x, w_pair[:, n * 256 : (n + 1) * 256])
            for p in range(PAIR):
                for k in range(2):
                    ybuf[g * PAIR + p, 2 * n + k] = y[p * T : (p + 1) * T, k * 128 : (k + 1) * 128]
            if n == 0:
                for p in range(PAIR):
                    far_hop(g * PAIR + p, g)

    def hops(g, hop):
        came(g, hop - 1)
        for p in range(PAIR):
            next_hop(g * PAIR + p, g, hop)

    begin(0)
    begin(1)
    rows_other = w_pair.at[pl.ds(256, 256)]
    pltpu.make_async_remote_copy(
        src_ref=rows_other,
        dst_ref=rows_other,
        send_sem=co_ss,
        recv_sem=co_rs,
        device_id=other,
        device_id_type=MESH,
    ).wait()
    out(0)
    begin(2)
    out(1)
    hops(0, 1)
    begin(3)
    for d in ORDER:
        send_return(d, 0)
    rt_recv[me] = return_lane(me)
    out(2)
    hops(1, 1)
    hops(0, 2)
    out(3)
    for g, hop in ((2, 1), (3, 1), (1, 2), (2, 2), (3, 2), (0, 3), (1, 3), (2, 3), (3, 3)):
        hops(g, hop)

    settle(rt_send, rt_recv, rt_ss, rt_rs)

    def leave(s):
        return pltpu.make_async_copy(new_state.at[s], new_state_out.at[s], out_s.at[0])

    def store(s, carry):
        source = jnp.int32(0)
        found = jnp.int32(0)
        for d in range(NC):
            hit = (serve_slot[d] == s) & (serve_live[d] == 1)
            source = jnp.where(hit, d, source)
            found = jnp.where(hit, 1, found)
        came = rt_recv[source].astype(F32)
        fresh = found == 1
        new_state[s] = jnp.where(fresh, came[: 2 * DK], state[s])
        convl[s] = jnp.where(fresh, came[2 * DK :], convl[s])
        leave(s).start()
        return carry

    lax.fori_loop(0, SLOTS, store, 0)
    for s in range(SLOTS):
        for i in range(3):
            for b in range(4):
                newcf[i, s : s + 1, b * 128 : (b + 1) * 128] = convl[s, i * 4 + b : i * 4 + b + 1, :]
    new_conv[...] = newcf[...].astype(BF16)

    for g in range(CONVS // PAIR):
        came(g, 3)
        for p in range(PAIR):
            j = g * PAIR + p
            total = ybuf[j, 4] + rrecv[2, j, 0].astype(F32) + rrecv[2, j, 1].astype(F32)
            layer[j] = total.astype(BF16)
        pair = pl.ds(g * PAIR, PAIR)
        pltpu.make_async_copy(layer.at[pair], layer_out.at[pair], out_s.at[1]).start()

    ring_copy(rsend0, rrecv0, 0, 0, 0).wait_send()
    ring_copy(rsend, rrecv, 0, 0, 1).wait_send()
    pltpu.make_async_remote_copy(
        src_ref=nrm,
        dst_ref=nrm_other,
        send_sem=nx_ss,
        recv_sem=nx_rs.at[0],
        device_id=other,
        device_id_type=MESH,
    ).wait_send()
    pltpu.make_async_copy(new_state, new_state_out, out_s.at[0]).wait()
    pltpu.make_async_copy(layer, layer_out, out_s.at[1]).wait()


def hand_on(layer_in, state_in, conv_in, layer_out, state_out, conv_out, layer, state, conv, came, gone):
    parts = [(layer_in, layer, layer_out), (conv_in, conv, conv_out)]
    for n in range(8):
        part = pl.ds(2 * n, 2)
        parts.append((state_in.at[part], state.at[part], state_out.at[part]))
    take = [pltpu.make_async_copy(a, b, came.at[n]) for n, (a, b, _) in enumerate(parts)]
    give = [pltpu.make_async_copy(b, c, gone.at[n]) for n, (_, b, c) in enumerate(parts)]
    for copy in take:
        copy.start()
    for here, there in zip(take, give):
        here.wait()
        there.start()
    for copy in give:
        copy.wait()


def local(
    hidden,
    lengths,
    owners,
    slot_ids,
    state_cache,
    conv_cache,
    w_qkvz,
    w_beta_alpha,
    conv_weight,
    decay_log,
    step_bias,
    norm_gain,
    w_out,
):
    vmem = pl.BlockSpec(memory_space=pltpu.VMEM)
    smem = pl.BlockSpec(memory_space=pltpu.SMEM)
    dma = pltpu.SemaphoreType.DMA
    far = pl.BlockSpec(memory_space=pl.ANY)
    hbm = pl.BlockSpec(memory_space=pltpu.HBM)
    results = (
        jax.ShapeDtypeStruct((CONVS, T, 128), BF16),
        jax.ShapeDtypeStruct((SLOTS, 2 * DK, T), F32),
        jax.ShapeDtypeStruct((3, SLOTS, CH), BF16),
    )
    worked = pl.pallas_call(
        kernel,
        out_shape=results,
        in_specs=[far, smem, smem, smem, far, vmem, far, vmem, vmem, smem, smem, vmem, far],
        out_specs=(far, far, vmem),
        scratch_shapes=[
            pltpu.VMEM((CONVS, T, 2048), BF16),
            pltpu.VMEM((SLOTS, 2 * DK, 128), F32),
            pltpu.VMEM((2048, 768), BF16),
            pltpu.VMEM((256, 2048), BF16),
            pltpu.VMEM((SLOTS, 2 * DK, 128), F32),
            pltpu.VMEM((CONVS, T, 128), BF16),
            dma((4,)),
            dma((2,)),
            pltpu.VMEM((SLOTS, 16, 128), F32),
            pltpu.VMEM((128, 2048), F32),
            pltpu.VMEM((CONVS, T, 768), BF16),
            pltpu.VMEM((CONVS, T, 128), F32),
            pltpu.SMEM((NC,), jnp.int32),
            pltpu.SMEM((NC,), jnp.int32),
            pltpu.VMEM((NC, 16, 128), BF16),
            pltpu.VMEM((NC, 16, 128), BF16),
            pltpu.VMEM((NC, 2 * DK, 128), BF16),
            pltpu.VMEM((NC, 2 * DK, 128), BF16),
            pltpu.VMEM((PREP, 8 + T, CH), F32),
            pltpu.VMEM((PREP, 16, 128), F32),
            pltpu.VMEM((2 * CONVS, 2 * T, DK), BF16),
            pltpu.VMEM((2 * CONVS, 2 * T, DK), BF16),
            pltpu.VMEM((2 * CONVS, T, DK), F32),
            pltpu.VMEM((CONVS, T, 2 * DK), F32),
            pltpu.VMEM((2 * CONVS, 8, 128), F32),
            pltpu.VMEM((CONVS, 2 * DK + 16, 128), BF16),
            pltpu.VMEM((CONVS, T, 2 * DK), BF16),
            pltpu.VMEM((NC, 2 * DK + 16, 128), BF16),
            pltpu.VMEM((NC, 2 * DK + 16, 128), BF16),
            pltpu.VMEM((CONVS, T, 2 * DK), BF16),
            pltpu.VMEM((512, 1024), BF16),
            pltpu.VMEM((CONVS, NZ, T, 128), F32),
            pltpu.VMEM((CONVS, 2, T // 2, 128), BF16),
            pltpu.VMEM((CONVS, 2, T // 2, 128), BF16),
            pltpu.VMEM((3, CONVS, 2, T, 128), BF16),
            pltpu.VMEM((3, CONVS, 2, T, 128), BF16),
            pltpu.VMEM((3, SLOTS, CH), F32),
            dma(()),
            dma(()),
            dma(()),
            dma(()),
            dma(()),
            dma(()),
            dma(()),
            dma((CONVS // PAIR,)),
            dma(()),
            dma(()),
            dma((2,)),
            dma((CONVS // PAIR, 4)),
        ],
        compiler_params=pltpu.CompilerParams(
            collective_id=0, has_side_effects=True, vmem_limit_bytes=56 * 1024 * 1024
        ),
    )(
        hidden,
        lengths,
        owners,
        slot_ids,
        state_cache.reshape(SLOTS, 2 * DK, 128),
        conv_cache.transpose(1, 2, 0, 3).reshape(3, SLOTS, CH),
        w_qkvz.reshape(2048, 768),
        w_beta_alpha.transpose(1, 2, 0).reshape(4, 2048),
        conv_weight.reshape(4, CH),
        decay_log,
        step_bias,
        norm_gain.reshape(1, 128),
        w_out,
    )
    layer_out, new_state, new_conv = pl.pallas_call(
        hand_on,
        out_shape=results,
        in_specs=[hbm, hbm, hbm],
        out_specs=(hbm, hbm, hbm),
        scratch_shapes=[pltpu.VMEM(r.shape, r.dtype) for r in results] + [dma((10,)), dma((10,))],
    )(*worked)
    return (
        layer_out,
        new_state.reshape(state_cache.shape),
        new_conv.reshape(3, 1, SLOTS, CH).transpose(2, 0, 1, 3),
    )


def solution(mesh):
    return jax.shard_map(
        local,
        mesh=mesh,
        in_specs=(
            P("cache", None, None),
            P(),
            P(),
            P(),
            P("cache", "tensor", None, None),
            P("cache", None, "tensor", None),
            P(None, "tensor", None),
            P(None, "tensor", None),
            P(None, "tensor", None),
            P("tensor"),
            P("tensor"),
            P(),
            P("tensor", None),
        ),
        out_specs=(
            P("cache", None, "tensor"),
            P("cache", "tensor", None, None),
            P("cache", None, "tensor", None),
        ),
        check_vma=False,
    )
```

```python
import functools
import math

import jax
import jax.numpy as jnp
from jax import lax
from jax.experimental import pallas as pl
from jax.experimental.pallas import tpu as pltpu
from jax.sharding import PartitionSpec as P

F32, BF16 = jnp.float32, jnp.bfloat16
MESH = pl.DeviceIdType.MESH

NC = 16
NZ = 8
CONVS = 8
T = 128
DK = 128
CH = 512
SLOTS = 16
EARLY = 8
PAIR = 2
STEP = 4
PREP = 8
ORDER = sorted(range(1, NC), key=lambda n: -(min(n // 4, 4 - n // 4) + min(n % 4, 4 - n % 4)))


def mm(a, b, ca=1, cb=0):
    return lax.dot_general(
        a.astype(BF16), b.astype(BF16), (((ca,), (cb,)), ((), ())), preferred_element_type=F32
    )


def silu(v):
    return v * (0.5 * jnp.tanh(0.5 * v) + 0.5)


def kernel(
    hidden_in,
    lengths,
    owners,
    slots,
    state_in,
    conv_cache,
    w_qkvz_in,
    w_ba,
    conv_weight,
    decay_log,
    step_bias,
    norm_gain,
    w_out_in,
    layer_out,
    new_state_out,
    new_conv,
    hidden,
    state,
    w_qkvz,
    w_out,
    new_state,
    layer,
    in_s,
    out_s,
    convl,
    wbp,
    proj,
    gate,
    serve_slot,
    serve_live,
    cv_send,
    cv_recv,
    st_send,
    st_recv,
    ext,
    tail_tmp,
    wq,
    pk,
    u0,
    zg,
    eg_end,
    fin,
    nrm,
    rt_send,
    rt_recv,
    nrm_other,
    w_pair,
    ybuf,
    rsend0,
    rrecv0,
    rsend,
    rrecv,
    newcf,
    cv_ss,
    cv_rs,
    st_ss,
    st_rs,
    rt_ss,
    rt_rs,
    nx_ss,
    nx_rs,
    co_ss,
    co_rs,
    ri_ss,
    ri_rs,
):
    me = lax.axis_index("cache")
    tt = lax.axis_index("tensor")
    z = tt // 2
    c = lax.rem(tt, 2)
    other = (me, z * 2 + 1 - c)
    up = (me, lax.rem(z + 1, NZ) * 2 + c)
    down = (me, lax.rem(z + NZ - 1, NZ) * 2 + c)

    def ahead(n):
        return lax.rem(me // 4 + n // 4, 4) * 4 + lax.rem(lax.rem(me, 4) + lax.rem(n, 4), 4)

    loads = [
        pltpu.make_async_copy(src, dst, in_s.at[n])
        for n, (src, dst) in enumerate(
            [(state_in, state), (w_out_in, w_out), (w_qkvz_in, w_qkvz), (hidden_in, hidden)]
        )
    ]
    for load in loads:
        load.start()

    barrier = pltpu.get_barrier_semaphore()

    def greet(d, carry):
        pl.semaphore_signal(barrier, inc=1, device_id=(ahead(d), tt), device_id_type=MESH)
        return carry

    for d in ORDER:
        greet(d, 0)
    for peer in (other, up, down):
        pl.semaphore_signal(barrier, inc=1, device_id=peer, device_id_type=MESH)
    newcf[...] = conv_cache[...].astype(F32)
    convl[...] = jnp.zeros_like(convl)
    for s in range(SLOTS):
        for i in range(3):
            for b in range(4):
                convl[s, i * 4 + b : i * 4 + b + 1, :] = newcf[i, s : s + 1, b * 128 : (b + 1) * 128]

    def cv_copy(d):
        peer = ahead(d)
        return pltpu.make_async_remote_copy(
            src_ref=cv_send.at[peer],
            dst_ref=cv_recv.at[me],
            send_sem=cv_ss,
            recv_sem=cv_rs,
            device_id=(peer, tt),
            device_id_type=MESH,
        )

    def st_copy(d):
        peer = ahead(d)
        return pltpu.make_async_remote_copy(
            src_ref=st_send.at[peer],
            dst_ref=st_recv.at[me],
            send_sem=st_ss,
            recv_sem=st_rs,
            device_id=(peer, tt),
            device_id_type=MESH,
        )

    def settle(sent, came, send_sem, recv_sem):
        lanes = pl.ds(0, NC - 1)
        pltpu.make_async_remote_copy(
            src_ref=sent.at[lanes],
            dst_ref=came.at[lanes],
            send_sem=send_sem,
            recv_sem=recv_sem,
            device_id=(ahead(1), tt),
            device_id_type=MESH,
        ).wait()

    def conv_lane(peer):
        slot = jnp.int32(0)
        live = jnp.int32(0)
        for j in range(CONVS):
            hit = owners[peer * CONVS + j] == me
            slot = jnp.where(hit, slots[peer * CONVS + j], slot)
            live = jnp.where(hit, 1, live)
        serve_slot[peer] = slot
        serve_live[peer] = live
        return convl[slot].astype(BF16)

    tail_tmp[...] = jnp.zeros_like(tail_tmp)

    def pack_conv(peer, carry):
        cv_send[peer] = conv_lane(peer)
        return carry

    lax.fori_loop(0, NC, pack_conv, 0)
    cv_recv[me] = cv_send[me]
    pl.semaphore_wait(barrier, NC - 1 + 3)

    def send_conv(d, carry):
        cv_copy(d).start()
        return carry

    for d in ORDER:
        send_conv(d, 0)

    loads[0].wait()

    for n, d in enumerate(ORDER):
        peer = ahead(d)
        st_send[peer] = state[serve_slot[peer]].astype(BF16)
        if n < EARLY:

            @pl.when(c == 0)
            def _(d=d):
                st_copy(d).start()
    st_recv[me] = state[serve_slot[me]].astype(BF16)

    def columns(r, core):
        return pl.ds(pl.multiple_of((lax.rem(z + 4 + r, NZ) * 2 + core) * 128, 128), 128)

    def weight_copy(r):
        return pltpu.make_async_remote_copy(
            src_ref=w_out.at[:, columns(r, 1 - c)],
            dst_ref=w_pair.at[pl.ds(256, 256), pl.ds(r * 128, 128)],
            send_sem=co_ss,
            recv_sem=co_rs,
            device_id=other,
            device_id_type=MESH,
        )

    settle(cv_send, cv_recv, cv_ss, cv_rs)

    for n, d in enumerate(ORDER):
        if n < EARLY:

            @pl.when(c == 1)
            def _(d=d):
                st_copy(d).start()
        else:
            st_copy(d).start()

    loads[1].wait()
    for r in range(NZ):
        weight_copy(r).start()
    for r in range(NZ):
        w_pair[0:256, r * 128 : (r + 1) * 128] = w_out[:, columns(r, c)]

    wbp[...] = jnp.zeros_like(wbp)
    wbp[0:4, :] = w_ba[...].astype(F32)
    loads[2].wait()
    loads[3].wait()

    def project(g, carry):
        x = hidden[pl.ds(g * STEP, STEP)].reshape(STEP * T, hidden.shape[-1])
        projected = mm(x, w_qkvz[...]).astype(BF16)
        gates = mm(x, wbp[...], 1, 1).astype(BF16).astype(F32)
        for p in range(STEP):
            proj[g * STEP + p] = projected[p * T : (p + 1) * T]
            gate[g * STEP + p] = gates[p * T : (p + 1) * T]
        return carry

    lax.fori_loop(0, CONVS // STEP, project, 0)

    rows = lax.broadcasted_iota(jnp.int32, (T, T), 0)
    cols = lax.broadcasted_iota(jnp.int32, (T, T), 1)
    lane = lax.broadcasted_iota(jnp.int32, (1, T), 1)
    pos = lax.broadcasted_iota(jnp.int32, (T, 1), 0)

    def prepare(g, carry):
        rate = jnp.exp(
            jnp.where(lane == 2, decay_log[0], jnp.where(lane == 3, decay_log[1], 0.0))
        )
        bias = jnp.where(lane == 2, step_bias[0], jnp.where(lane == 3, step_bias[1], 0.0))
        inclusive = rows >= cols
        strictly = rows > cols
        tri = jnp.where(inclusive, 1.0, 0.0)
        chains = []
        for p in range(PREP):
            j = g * PREP + p
            length = lengths[me * CONVS + j]
            owner = owners[me * CONVS + j]
            live = pos < length
            mixed = proj[j, :, :CH].astype(F32)
            z_part = proj[j, :, CH:].astype(F32)
            held = cv_recv[owner].astype(F32)
            for i in range(3):
                for b in range(4):
                    ext[p, 5 + i : 6 + i, b * 128 : (b + 1) * 128] = held[i * 4 + b : i * 4 + b + 1, :]
            ext[p, 8 : 8 + T, :] = mixed
            convolved = conv_weight[3:4, :].astype(F32) * mixed
            for i in range(3):
                convolved = convolved + conv_weight[i : i + 1, :].astype(F32) * ext[p, 5 + i : 5 + i + T, :]
            for i in range(3):
                row = ext[p, pl.ds(5 + length + i, 1), :]
                for b in range(4):
                    tail_tmp[p, i * 4 + b : i * 4 + b + 1, :] = row[:, b * 128 : (b + 1) * 128]
            fin[j, 2 * DK : 2 * DK + 16, :] = tail_tmp[p].astype(BF16)
            act = silu(convolved)
            q = act[:, :DK]
            k = act[:, DK : 2 * DK]
            q = q * lax.rsqrt(jnp.sum(q * q, axis=-1, keepdims=True) + 1e-06) * (1.0 / math.sqrt(DK))
            k = k * lax.rsqrt(jnp.sum(k * k, axis=-1, keepdims=True) + 1e-06)
            zg[j] = jnp.where(
                live,
                silu(z_part) * jnp.concatenate([norm_gain[...], norm_gain[...]], axis=1),
                0.0,
            )
            raw = gate[j]
            beta = jnp.where(live, 0.5 * jnp.tanh(0.5 * raw) + 0.5, 0.0)
            shifted = raw + bias
            decay = jnp.where(
                live,
                -rate * (jnp.maximum(shifted, 0.0) + jnp.log1p(jnp.exp(-jnp.abs(shifted)))),
                0.0,
            )
            total = jnp.dot(tri, decay, precision=lax.Precision.HIGHEST, preferred_element_type=F32)
            total_rows = total.T
            qk = mm(jnp.concatenate([k, q], axis=0), k, 1, 1)
            k_t = k.T
            for h in range(2):
                gc = total[:, 2 + h : 3 + h]
                gr = total_rows[2 + h : 3 + h, :]
                g_end = gr[:, T - 1 : T]
                bc = beta[:, h : h + 1]
                gap = jnp.where(inclusive, jnp.exp(jnp.where(inclusive, gc - gr, 0.0)), 0.0)
                lower = jnp.where(strictly, bc * qk[:T] * gap, 0.0)
                grow = jnp.exp(gc)
                wq[2 * j + h, T:, :] = (q * grow).astype(BF16)
                pk[2 * j + h, :T, :] = (qk[T:] * gap).astype(BF16)
                pk[2 * j + h, T:, :] = (k_t * jnp.exp(g_end - gr)).astype(BF16)
                eg_end[2 * j + h] = jnp.broadcast_to(jnp.exp(g_end), (8, T))
                right = jnp.concatenate(
                    [(bc * grow * k), bc * act[:, 2 * DK + h * T : 2 * DK + (h + 1) * T]], axis=1
                ).astype(BF16)
                chains.append((2 * j + h, lower, right))
        inverse = [
            jnp.where(rows == cols, 1.0, 0.0) - jnp.where(rows // 2 == cols // 2, low, 0.0)
            for _, low, _ in chains
        ]
        span = 2
        while span < T:
            block = (rows // (4 * span) == cols // (4 * span)) & (rows // span != cols // span)
            nil = [mm(inv, jnp.where(block, low, 0.0)) for (_, low, _), inv in zip(chains, inverse)]
            square = [mm(n, n) for n in nil]
            first = [inv - mm(n, inv) for n, inv in zip(nil, inverse)]
            inverse = [f + mm(q, f) for q, f in zip(square, first)]
            span *= 4
        for (at, _, right), inv in zip(chains, inverse):
            solved = mm(inv, right)
            wq[at, :T, :] = solved[:, :DK].astype(BF16)
            u0[at] = solved[:, DK:]
        return carry

    lax.fori_loop(0, CONVS // PREP, prepare, 0)

    settle(st_send, st_recv, st_ss, st_rs)

    def finish(g, carry):
        for p in range(PAIR):
            j = g * PAIR + p
            owner = owners[me * CONVS + j]
            for h in range(2):
                at = 2 * j + h
                memory = st_recv[owner, h * DK : (h + 1) * DK, :]
                seen = mm(wq[at], memory)
                update = u0[at] - seen[:T]
                given = mm(pk[at], update)
                core = seen[T:] + given[:T]
                after = eg_end[at][0:1, :] * memory.astype(F32) + given[T:]
                fin[j, h * DK : (h + 1) * DK, :] = after.astype(BF16)
                scale = lax.rsqrt(jnp.mean(core * core, axis=-1, keepdims=True) + 1e-06)
                nrm[j, :, h * DK : (h + 1) * DK] = (
                    core * scale * zg[j, :, h * DK : (h + 1) * DK]
                ).astype(BF16)
        return carry

    def rt_copy(d):
        peer = ahead(d)
        return pltpu.make_async_remote_copy(
            src_ref=rt_send.at[peer],
            dst_ref=rt_recv.at[me],
            send_sem=rt_ss,
            recv_sem=rt_rs,
            device_id=(peer, tt),
            device_id_type=MESH,
        )

    def return_lane(peer):
        pick = jnp.int32(0)
        for j in range(CONVS):
            pick = jnp.where(owners[me * CONVS + j] == peer, j, pick)
        return fin[pick]

    def send_return(d, carry):
        peer = ahead(d)
        rt_send[peer] = return_lane(peer)
        rt_copy(d).start()
        return carry

    def norm_copy(g):
        pair = pl.ds(g * PAIR, PAIR)
        return pltpu.make_async_remote_copy(
            src_ref=nrm.at[pair],
            dst_ref=nrm_other.at[pair],
            send_sem=nx_ss,
            recv_sem=nx_rs.at[g],
            device_id=other,
            device_id_type=MESH,
        )

    def ring_copy(src, dst, way, g, hop):
        return pltpu.make_async_remote_copy(
            src_ref=src,
            dst_ref=dst,
            send_sem=ri_ss.at[min(hop, 1)],
            recv_sem=ri_rs.at[g, hop],
            device_id=up if way == 0 else down,
            device_id_type=MESH,
        )

    half = T // 2

    def far_hop(j, g):
        far = ybuf[j, 0].astype(BF16)
        for way in (0, 1):
            rsend0[j, way] = far[way * half : (way + 1) * half]
            ring_copy(rsend0.at[j, way], rrecv0.at[j, way], way, g, 0).start()

    def came(g, hop):
        pair = pl.ds(g * PAIR, PAIR)
        ref = rrecv0.at[pair] if hop == 0 else rrecv.at[hop - 1, pair]
        ring_copy(ref, ref, 0, g, hop).wait_recv()

    def next_hop(j, g, hop):
        for way in (0, 1):
            mine = ybuf[j, NZ - hop if way == 0 else hop]
            if hop == 1:
                keep = slice(way * half, (way + 1) * half)
                alone = slice((1 - way) * half, (2 - way) * half)
                rsend[0, j, way, keep, :] = (mine[keep] + rrecv0[j, way].astype(F32)).astype(BF16)
                rsend[0, j, way, alone, :] = mine[alone].astype(BF16)
            else:
                rsend[hop - 1, j, way] = (mine + rrecv[hop - 2, j, way].astype(F32)).astype(BF16)
            ring_copy(rsend.at[hop - 1, j, way], rrecv.at[hop - 1, j, way], way, g, hop).start()

    def begin(g):
        finish(g, 0)
        norm_copy(g).start()

    def out(g):
        norm_copy(g).wait_recv()
        pair = pl.ds(g * PAIR, PAIR)
        x = jnp.concatenate([nrm[pair].reshape(PAIR * T, 256), nrm_other[pair].reshape(PAIR * T, 256)], axis=1)
        for n in range(NZ // 2):
            y = mm(x, w_pair[:, n * 256 : (n + 1) * 256])
            for p in range(PAIR):
                for k in range(2):
                    ybuf[g * PAIR + p, 2 * n + k] = y[p * T : (p + 1) * T, k * 128 : (k + 1) * 128]
            if n == 0:
                for p in range(PAIR):
                    far_hop(g * PAIR + p, g)

    def hops(g, hop):
        came(g, hop - 1)
        for p in range(PAIR):
            next_hop(g * PAIR + p, g, hop)

    begin(0)
    begin(1)
    rows_other = w_pair.at[pl.ds(256, 256)]
    pltpu.make_async_remote_copy(
        src_ref=rows_other,
        dst_ref=rows_other,
        send_sem=co_ss,
        recv_sem=co_rs,
        device_id=other,
        device_id_type=MESH,
    ).wait()
    out(0)
    begin(2)
    out(1)
    hops(0, 1)
    begin(3)
    for d in ORDER:
        send_return(d, 0)
    rt_recv[me] = return_lane(me)
    out(2)
    hops(1, 1)
    hops(0, 2)
    out(3)
    for g, hop in ((2, 1), (3, 1), (1, 2), (2, 2), (3, 2), (0, 3), (1, 3), (2, 3), (3, 3)):
        hops(g, hop)

    settle(rt_send, rt_recv, rt_ss, rt_rs)

    def leave(s):
        return pltpu.make_async_copy(new_state.at[s], new_state_out.at[s], out_s.at[0])

    def store(s, carry):
        source = jnp.int32(0)
        found = jnp.int32(0)
        for d in range(NC):
            hit = (serve_slot[d] == s) & (serve_live[d] == 1)
            source = jnp.where(hit, d, source)
            found = jnp.where(hit, 1, found)
        came = rt_recv[source].astype(F32)
        fresh = found == 1
        new_state[s] = jnp.where(fresh, came[: 2 * DK], state[s])
        convl[s] = jnp.where(fresh, came[2 * DK :], convl[s])
        leave(s).start()
        return carry

    lax.fori_loop(0, SLOTS, store, 0)
    for s in range(SLOTS):
        for i in range(3):
            for b in range(4):
                newcf[i, s : s + 1, b * 128 : (b + 1) * 128] = convl[s, i * 4 + b : i * 4 + b + 1, :]
    new_conv[...] = newcf[...].astype(BF16)

    for g in range(CONVS // PAIR):
        came(g, 3)
        for p in range(PAIR):
            j = g * PAIR + p
            total = ybuf[j, 4] + rrecv[2, j, 0].astype(F32) + rrecv[2, j, 1].astype(F32)
            layer[j] = total.astype(BF16)
        pair = pl.ds(g * PAIR, PAIR)
        pltpu.make_async_copy(layer.at[pair], layer_out.at[pair], out_s.at[1]).start()

    ring_copy(rsend0, rrecv0, 0, 0, 0).wait_send()
    ring_copy(rsend, rrecv, 0, 0, 1).wait_send()
    pltpu.make_async_remote_copy(
        src_ref=nrm,
        dst_ref=nrm_other,
        send_sem=nx_ss,
        recv_sem=nx_rs.at[0],
        device_id=other,
        device_id_type=MESH,
    ).wait_send()
    pltpu.make_async_copy(new_state, new_state_out, out_s.at[0]).wait()
    pltpu.make_async_copy(layer, layer_out, out_s.at[1]).wait()


def hand_on(layer_in, state_in, conv_in, layer_out, state_out, conv_out, layer, state, conv, came, gone):
    parts = [(layer_in, layer, layer_out), (conv_in, conv, conv_out)]
    for n in range(8):
        part = pl.ds(2 * n, 2)
        parts.append((state_in.at[part], state.at[part], state_out.at[part]))
    take = [pltpu.make_async_copy(a, b, came.at[n]) for n, (a, b, _) in enumerate(parts)]
    give = [pltpu.make_async_copy(b, c, gone.at[n]) for n, (_, b, c) in enumerate(parts)]
    for copy in take:
        copy.start()
    for here, there in zip(take, give):
        here.wait()
        there.start()
    for copy in give:
        copy.wait()


def local(
    hidden,
    lengths,
    owners,
    slot_ids,
    state_cache,
    conv_cache,
    w_qkvz,
    w_beta_alpha,
    conv_weight,
    decay_log,
    step_bias,
    norm_gain,
    w_out,
):
    vmem = pl.BlockSpec(memory_space=pltpu.VMEM)
    smem = pl.BlockSpec(memory_space=pltpu.SMEM)
    dma = pltpu.SemaphoreType.DMA
    far = pl.BlockSpec(memory_space=pl.ANY)
    hbm = pl.BlockSpec(memory_space=pltpu.HBM)
    results = (
        jax.ShapeDtypeStruct((CONVS, T, 128), BF16),
        jax.ShapeDtypeStruct((SLOTS, 2 * DK, T), F32),
        jax.ShapeDtypeStruct((3, SLOTS, CH), BF16),
    )
    worked = pl.pallas_call(
        kernel,
        out_shape=results,
        in_specs=[far, smem, smem, smem, far, vmem, far, vmem, vmem, smem, smem, vmem, far],
        out_specs=(far, far, vmem),
        scratch_shapes=[
            pltpu.VMEM((CONVS, T, 2048), BF16),
            pltpu.VMEM((SLOTS, 2 * DK, 128), F32),
            pltpu.VMEM((2048, 768), BF16),
            pltpu.VMEM((256, 2048), BF16),
            pltpu.VMEM((SLOTS, 2 * DK, 128), F32),
            pltpu.VMEM((CONVS, T, 128), BF16),
            dma((4,)),
            dma((2,)),
            pltpu.VMEM((SLOTS, 16, 128), F32),
            pltpu.VMEM((128, 2048), F32),
            pltpu.VMEM((CONVS, T, 768), BF16),
            pltpu.VMEM((CONVS, T, 128), F32),
            pltpu.SMEM((NC,), jnp.int32),
            pltpu.SMEM((NC,), jnp.int32),
            pltpu.VMEM((NC, 16, 128), BF16),
            pltpu.VMEM((NC, 16, 128), BF16),
            pltpu.VMEM((NC, 2 * DK, 128), BF16),
            pltpu.VMEM((NC, 2 * DK, 128), BF16),
            pltpu.VMEM((PREP, 8 + T, CH), F32),
            pltpu.VMEM((PREP, 16, 128), F32),
            pltpu.VMEM((2 * CONVS, 2 * T, DK), BF16),
            pltpu.VMEM((2 * CONVS, 2 * T, DK), BF16),
            pltpu.VMEM((2 * CONVS, T, DK), F32),
            pltpu.VMEM((CONVS, T, 2 * DK), F32),
            pltpu.VMEM((2 * CONVS, 8, 128), F32),
            pltpu.VMEM((CONVS, 2 * DK + 16, 128), BF16),
            pltpu.VMEM((CONVS, T, 2 * DK), BF16),
            pltpu.VMEM((NC, 2 * DK + 16, 128), BF16),
            pltpu.VMEM((NC, 2 * DK + 16, 128), BF16),
            pltpu.VMEM((CONVS, T, 2 * DK), BF16),
            pltpu.VMEM((512, 1024), BF16),
            pltpu.VMEM((CONVS, NZ, T, 128), F32),
            pltpu.VMEM((CONVS, 2, T // 2, 128), BF16),
            pltpu.VMEM((CONVS, 2, T // 2, 128), BF16),
            pltpu.VMEM((3, CONVS, 2, T, 128), BF16),
            pltpu.VMEM((3, CONVS, 2, T, 128), BF16),
            pltpu.VMEM((3, SLOTS, CH), F32),
            dma(()),
            dma(()),
            dma(()),
            dma(()),
            dma(()),
            dma(()),
            dma(()),
            dma((CONVS // PAIR,)),
            dma(()),
            dma(()),
            dma((2,)),
            dma((CONVS // PAIR, 4)),
        ],
        compiler_params=pltpu.CompilerParams(
            collective_id=0, has_side_effects=True, vmem_limit_bytes=56 * 1024 * 1024
        ),
    )(
        hidden,
        lengths,
        owners,
        slot_ids,
        state_cache.reshape(SLOTS, 2 * DK, 128),
        conv_cache.transpose(1, 2, 0, 3).reshape(3, SLOTS, CH),
        w_qkvz.reshape(2048, 768),
        w_beta_alpha.transpose(1, 2, 0).reshape(4, 2048),
        conv_weight.reshape(4, CH),
        decay_log,
        step_bias,
        norm_gain.reshape(1, 128),
        w_out,
    )
    layer_out, new_state, new_conv = pl.pallas_call(
        hand_on,
        out_shape=results,
        in_specs=[hbm, hbm, hbm],
        out_specs=(hbm, hbm, hbm),
        scratch_shapes=[pltpu.VMEM(r.shape, r.dtype) for r in results] + [dma((10,)), dma((10,))],
    )(*worked)
    return (
        layer_out,
        new_state.reshape(state_cache.shape),
        new_conv.reshape(3, 1, SLOTS, CH).transpose(2, 0, 1, 3),
    )


def solution(mesh):
    return jax.shard_map(
        local,
        mesh=mesh,
        in_specs=(
            P("cache", None, None),
            P(),
            P(),
            P(),
            P("cache", "tensor", None, None),
            P("cache", None, "tensor", None),
            P(None, "tensor", None),
            P(None, "tensor", None),
            P(None, "tensor", None),
            P("tensor"),
            P("tensor"),
            P(),
            P("tensor", None),
        ),
        out_specs=(
            P("cache", None, "tensor"),
            P("cache", "tensor", None, None),
            P("cache", None, "tensor", None),
        ),
        check_vma=False,
    )
```
